32 devices in a mesh: blk: 8 (over z, x), head: 4 (over y, core).
Axes of the slice: x: 2, y: 2, z: 4, core: 2. Of those that a mesh axis runs over, the one named last changes fastest.
Arguments:
- block_in: bfloat16 [4, 1024, 2048], P('head', 'blk'), may hold values from -6 to 6
- lengths: int32 [4], replicated, may hold values from 256 to 1024, as said below
- out_cot: bfloat16 [4, 1024, 2048], P('head', 'blk'), may hold values from -6 to 6
- ln1_gain: float32 [2048], replicated, may hold values from 0.5 to 1.5
- ln1_bias: float32 [2048], replicated, may hold values from -1 to 1
- w_q: bfloat16 [2048, 2048], P('blk', 'head'), may hold values from -0.1875 to 0.1875
- b_q: float32 [2048], replicated, may hold values from -1 to 1
- w_kv: bfloat16 [2048, 256], replicated, may hold values from -0.1875 to 0.1875
- b_v: float32 [128], replicated, may hold values from -1 to 1
- w_out: bfloat16 [2048, 2048], P('blk', 'head'), may hold values from -0.75 to 0.75
- b_out: float32 [2048], replicated, may hold values from -1 to 1
- ln2_gain: float32 [2048], replicated, may hold values from 0.5 to 1.5
- ln2_bias: float32 [2048], replicated, may hold values from -1 to 1
- w_up: bfloat16 [2048, 8192], P('blk', 'head'), may hold values from -0.125 to 0.125
- b_up: float32 [8192], replicated, may hold values from -1 to 1
- w_down: bfloat16 [2048, 8192], P('blk', 'head'), may hold values from -0.0625 to 0.0625
- b_down: float32 [2048], replicated, may hold values from -1 to 1
Outputs:
- block_out: bfloat16 [4, 1024, 2048], P('head', 'blk')
- grad_in: float32 [4, 1024, 2048], P('head', 'blk')
- g_ln1_gain: float32 [2048], replicated
- g_ln1_bias: float32 [2048], replicated
- g_w_q: float32 [2048, 2048], P('blk', 'head')
- g_b_q: float32 [2048], replicated
- g_w_kv: float32 [2048, 256], replicated
- g_b_v: float32 [128], replicated
- g_w_out: float32 [2048, 2048], P('blk', 'head')
- g_b_out: float32 [2048], replicated
- g_ln2_gain: float32 [2048], replicated
- g_ln2_bias: float32 [2048], replicated
- g_w_up: float32 [2048, 8192], P('blk', 'head')
- g_b_up: float32 [8192], replicated
- g_w_down: float32 [2048, 8192], P('blk', 'head')
- g_b_down: float32 [2048], replicated
The draws below stay inside these ranges and needn't reach their ends.
Inputs may be any that keep to these rules, and one draw needn't show every extreme that they name: `lengths`: one slot, drawn from the seed, has exactly 1024 valid positions; each other slot has between 256 and 1024.
All inputs are finite; a program needn't handle non-finite values.
Results may differ from the reference program's by a relative error of at most 0.02.
Values may be sent and summed in bfloat16 or wider, within the bound.
No kernel may reach another device: no remote copies, remote signals or barrier semaphores. Data moves between devices by JAX's collectives and lax.ppermute only.
A program may use at most 192 MiB of HBM per device.

```python
import jax
import jax.numpy as jnp
from jax import lax

D = 2048
FF = 8192
HEADS = 16
HEAD_DIM = 128
SLOTS = 4
SEQ = 1024


def draw_lengths(key, part):
    key = jax.random.fold_in(key, 11)
    draw_key, pick_key = jax.random.split(key)
    others = jax.random.randint(draw_key, (SLOTS,), SEQ // 4, SEQ + 1)
    longest = jax.random.randint(pick_key, (), 0, SLOTS)
    return jnp.where(jnp.arange(SLOTS) == longest, SEQ, others).astype(jnp.int32)


def shard_levels(key, dims, shards, smallest, largest):
    def one(dim, parts):
        steps = jax.random.uniform(jax.random.fold_in(jax.random.fold_in(key, 6), dim), (parts,), jnp.float32, smallest / len(shards), largest / len(shards))
        return jnp.repeat(jnp.exp(steps), dims[dim] // parts).reshape((-1,) + (1,) * (len(dims) - dim - 1))

    level = one(*shards[0])
    for cut in shards[1:]:
        level = level * one(*cut)
    return level


def gaussian(stream_key, extent, scale, reach, pieces=(), kind=jnp.bfloat16):
    drawn = scale * jax.random.normal(stream_key, extent, jnp.float32)
    if pieces:
        drawn = drawn * shard_levels(stream_key, extent, pieces, -0.22, 0.18)
    return jnp.clip(drawn, -reach, reach).astype(kind)


def setup_inputs(seed: int = 0) -> dict:
    key_list = jax.random.split(jax.random.key(seed), 18)
    return {
        "block_in": gaussian(key_list[0], (SLOTS, SEQ, D), 1.0, 6.0, ((0, 4), (1, 8))),
        "lengths": draw_lengths(jax.random.fold_in(key_list[17], 71), 0),
        "out_cot": gaussian(key_list[2], (SLOTS, SEQ, D), 1.0, 6.0, ((0, 4), (1, 8))),
        "ln1_gain": jnp.clip(1.0 + 0.1 * jax.random.normal(key_list[3], (D,), jnp.float32), 0.5, 1.5),
        "ln1_bias": gaussian(key_list[4], (D,), 0.2, 1.0, (), jnp.float32),
        "w_q": gaussian(key_list[5], (D, D), (D // 2) ** -0.5, 0.1875, ((0, 8), (1, 4))),
        "b_q": gaussian(key_list[6], (D,), 0.2, 1.0, (), jnp.float32),
        "w_kv": gaussian(key_list[7], (D, 2 * HEAD_DIM), (D // 2) ** -0.5, 0.1875),
        "b_v": gaussian(key_list[8], (HEAD_DIM,), 0.2, 1.0, (), jnp.float32),
        "w_out": gaussian(key_list[9], (D, D), (D // 32) ** -0.5, 0.75, ((0, 8), (1, 4))),
        "b_out": gaussian(key_list[10], (D,), 0.2, 1.0, (), jnp.float32),
        "ln2_gain": jnp.clip(1.0 + 0.1 * jax.random.normal(key_list[11], (D,), jnp.float32), 0.5, 1.5),
        "ln2_bias": gaussian(key_list[12], (D,), 0.2, 1.0, (), jnp.float32),
        "w_up": gaussian(key_list[13], (D, FF), D ** -0.5, 0.125, ((0, 8), (1, 4))),
        "b_up": gaussian(key_list[14], (FF,), 0.2, 1.0, (), jnp.float32),
        "w_down": gaussian(key_list[15], (D, FF), FF ** -0.5, 0.0625, ((0, 8), (1, 4))),
        "b_down": gaussian(key_list[16], (D,), 0.2, 1.0, (), jnp.float32),
    }


@jax.custom_vjp
def low(v):
    return lax.optimization_barrier(v.astype(jnp.bfloat16)).astype(jnp.float32)

@jax.custom_vjp
def low_back(v):
    return v

def low_keep(v):
    return (low(v), None)

def low_pass(kept, grad):
    return (grad,)

def back_keep(v):
    return (v, None)

def back_low(kept, grad):
    return (low(grad),)
low.defvjp(low_keep, low_pass)
low_back.defvjp(back_keep, back_low)
HIGHEST = lax.Precision.HIGHEST
EPSILON = 1e-05

def layer_norm(values, gain, bias):
    center = values - lax.optimization_barrier(jnp.mean(values, axis=-1, keepdims=True))
    spread = lax.optimization_barrier(jnp.mean(center * center, axis=-1, keepdims=True))
    return center * lax.rsqrt(spread + EPSILON) * gain + bias

def matmul(left, right):
    return jnp.dot(left, right, precision=HIGHEST)

def attend(queries, keys, values, length):
    block_rows = min(512, SEQ)
    block_count = SEQ // block_rows
    score_scale = HEAD_DIM ** (-0.5)
    key_pos = jnp.arange(SEQ, dtype=jnp.int32)

    @jax.checkpoint
    def one_block(item):
        query_block, start = item
        raw = jnp.einsum('qhd,kd->hqk', query_block, keys, precision=HIGHEST) * score_scale
        scores = low_back(raw)
        query_pos = start + jnp.arange(block_rows, dtype=jnp.int32)
        allowed = (key_pos[None, :] <= query_pos[:, None]) & (key_pos[None, :] < length)
        masked = jnp.where(allowed[None], scores, -1e+30)
        log_total = jax.nn.logsumexp(masked, axis=-1, keepdims=True)
        probs = jnp.where(allowed[None], jnp.exp(masked - log_total), 0.0)
        return jnp.einsum('hqk,kd->qhd', low(probs), values, precision=HIGHEST)
    starts = jnp.arange(block_count, dtype=jnp.int32) * block_rows
    outputs = lax.map(one_block, (queries.reshape(block_count, block_rows, HEADS, HEAD_DIM), starts))
    return outputs.reshape(SEQ, HEADS * HEAD_DIM)

def forward_slot(inputs, length, params):
    gain_one, bias_one, weight_q, bias_q, weight_kv, bias_v, weight_out, bias_out, gain_two, bias_two, weight_up, bias_up, weight_down, bias_down = params
    attn_in = low(layer_norm(inputs, gain_one, bias_one))
    queries = low(low_back(matmul(attn_in, weight_q) + bias_q))
    value_bias = jnp.concatenate([jnp.zeros_like(bias_v), bias_v])
    key_value = low(low_back(matmul(attn_in, weight_kv) + value_bias))
    mixed = attend(queries.reshape(SEQ, HEADS, HEAD_DIM), key_value[:, :HEAD_DIM], key_value[:, HEAD_DIM:], length)
    mixed = low(low_back(mixed))
    hidden_res = inputs + low_back(matmul(mixed, weight_out.T)) + bias_out
    ffn_in = low(layer_norm(hidden_res, gain_two, bias_two))
    up_full = low_back(matmul(ffn_in, weight_up) + bias_up)
    activated = low(jax.nn.gelu(up_full, approximate=True))
    return hidden_res + low_back(matmul(activated, weight_down.T)) + bias_down

def reference(block_in, lengths, out_cot, ln1_gain, ln1_bias, w_q, b_q, w_kv, b_v, w_out, b_out, ln2_gain, ln2_bias, w_up, b_up, w_down, b_down):
    params = tuple((item.astype(jnp.float32) for item in (ln1_gain, ln1_bias, w_q, b_q, w_kv, b_v, w_out, b_out, ln2_gain, ln2_bias, w_up, b_up, w_down, b_down)))

    def step(totals, item):
        inputs, cotangent, length = item
        valid = (jnp.arange(SEQ, dtype=jnp.int32) < length)[:, None]

        def slot_fn(values, *weights):
            return forward_slot(values, length, weights)
        outputs, pull = jax.vjp(slot_fn, inputs.astype(jnp.float32), *params)
        grads = pull(jnp.where(valid, cotangent.astype(jnp.float32), 0.0))
        totals = tuple((total + grad for total, grad in zip(totals, grads[1:])))
        return (totals, (outputs.astype(jnp.bfloat16), grads[0]))
    initial = tuple((jnp.zeros_like(item) for item in params))
    totals, (outputs, input_grad) = lax.scan(step, initial, (block_in, out_cot, lengths))
    return (outputs, input_grad, totals[0], totals[1], totals[2], totals[3], totals[4], totals[5], totals[6], totals[7], totals[8], totals[9], totals[10], totals[11], totals[12], totals[13])
```

```python
from functools import partial

import jax
import jax.numpy as jnp
from jax import lax
from jax.experimental import pallas as pl
from jax.experimental.pallas import tpu as pltpu
from jax.sharding import PartitionSpec as P

HEADS = 16
HEAD_DIM = 128
EPSILON = 1e-05
SCALE = HEAD_DIM ** (-0.5)
LOW = jnp.bfloat16


def layer_norm(values, gain, bias):
    center = values - jnp.mean(values, axis=-1, keepdims=True)
    spread = jnp.mean(center * center, axis=-1, keepdims=True)
    return center * lax.rsqrt(spread + EPSILON) * gain + bias


def plain_dot(left, right):
    return jnp.dot(left, right, preferred_element_type=jnp.float32)


def row_dot(left, right):
    return lax.dot_general(
        left, right, (((0,), (0,)), ((), ())), preferred_element_type=jnp.float32
    )


def col_dot(left, right):
    return lax.dot_general(
        left, right, (((1,), (1,)), ((), ())), preferred_element_type=jnp.float32
    )


def wide(values):
    return values.astype(jnp.float32)


def low(values):
    return values.astype(LOW)


def rounded(values):
    return lax.reduce_precision(values, 8, 7)


def flip(values, blk_bits=0, head_bits=0):
    blk_count = lax.axis_size("blk")
    head_count = lax.axis_size("head")
    pairs = [
        (b * head_count + h, (b ^ blk_bits) * head_count + (h ^ head_bits))
        for b in range(blk_count)
        for h in range(head_count)
    ]
    return lax.ppermute(values, ("blk", "head"), pairs)


def in_order(own, other, index, axis):
    first = index == 0
    return jnp.stack([jnp.where(first, own, other), jnp.where(first, other, own)], axis=axis)


def tie(*values):
    return lax.optimization_barrier(values)


def take(values, index, axis):
    return lax.dynamic_index_in_dim(values, index, axis, keepdims=False)


def stacked(ref, heads):
    return jnp.concatenate(
        [ref[:, h * HEAD_DIM : (h + 1) * HEAD_DIM] for h in range(heads)], axis=0
    )


def probabilities(query, key, key_pos, start, length, seq_dev):
    raw = col_dot(query, key) * SCALE
    row = lax.broadcasted_iota(jnp.int32, (query.shape[0], 1), 0)
    row_pos = start + row % seq_dev
    limit = jnp.minimum(row_pos, length - 1)
    masked = jnp.where(key_pos <= limit, raw, -1e30)
    weights = jnp.exp(masked - jnp.max(masked, axis=-1, keepdims=True))
    return weights * (1.0 / jnp.sum(weights, axis=-1, keepdims=True))


def forward_kernel(heads, scalars, q_ref, kv_ref, pos_ref, o_ref):
    seq_dev = q_ref.shape[0]
    key = kv_ref[0, :, :HEAD_DIM]
    value = kv_ref[0, :, HEAD_DIM:]
    prob = probabilities(
        stacked(q_ref, heads),
        key,
        pos_ref[...],
        scalars[0],
        scalars[1 + pl.program_id(0)],
        seq_dev,
    )
    out = plain_dot(prob.astype(LOW), value).astype(LOW)
    for h in range(heads):
        o_ref[:, h * HEAD_DIM : (h + 1) * HEAD_DIM] = out[h * seq_dev : (h + 1) * seq_dev]


def backward_kernel(heads, scalars, q_ref, go_ref, kv_ref, pos_ref, gq_ref, gkv_ref):
    seq_dev = q_ref.shape[0]
    key = kv_ref[0, :, :HEAD_DIM]
    value = kv_ref[0, :, HEAD_DIM:]
    query = stacked(q_ref, heads)
    grad = stacked(go_ref, heads)
    prob = probabilities(
        query,
        key,
        pos_ref[...],
        scalars[0],
        scalars[1 + pl.program_id(0)],
        seq_dev,
    )
    prob_low = prob.astype(LOW)
    prob_grad = col_dot(grad, value)
    delta = jnp.sum(wide(prob_low) * prob_grad, axis=-1, keepdims=True)
    score_grad = (prob * (prob_grad - delta)).astype(LOW)
    out = (plain_dot(score_grad, key) * SCALE).astype(LOW)
    for h in range(heads):
        gq_ref[:, h * HEAD_DIM : (h + 1) * HEAD_DIM] = out[h * seq_dev : (h + 1) * seq_dev]
    key_grad = row_dot(score_grad, query) * SCALE
    value_grad = row_dot(prob_low, grad)

    @pl.when(pl.program_id(1) == 0)
    def _():
        gkv_ref[0, :, :HEAD_DIM] = key_grad
        gkv_ref[0, :, HEAD_DIM:] = value_grad

    @pl.when(pl.program_id(1) > 0)
    def _():
        gkv_ref[0, :, :HEAD_DIM] += key_grad
        gkv_ref[0, :, HEAD_DIM:] += value_grad


def attention_call(kernel, outs, scalars, rows, keys, key_pos, seq_dev, flops):
    slots, key_count, _ = keys.shape
    heads_dev = rows[0].shape[1] // HEAD_DIM
    heads = max(1, min(heads_dev, heads_dev * 1024 // key_count))
    row_spec = pl.BlockSpec((seq_dev, heads * HEAD_DIM), lambda s, g, *_: (s, g))
    key_spec = pl.BlockSpec((1, key_count, 2 * HEAD_DIM), lambda s, g, *_: (s, 0, 0))
    pos_spec = pl.BlockSpec((1, key_count), lambda s, g, *_: (0, 0))
    shapes = {
        "row": (jax.ShapeDtypeStruct(rows[0].shape, LOW), row_spec),
        "key": (jax.ShapeDtypeStruct(keys.shape, jnp.float32), key_spec),
    }
    return pl.pallas_call(
        partial(kernel, heads),
        grid_spec=pltpu.PrefetchScalarGridSpec(
            num_scalar_prefetch=1,
            grid=(slots, heads_dev // heads),
            in_specs=[row_spec] * len(rows) + [key_spec, pos_spec],
            out_specs=[shapes[o][1] for o in outs],
        ),
        out_shape=[shapes[o][0] for o in outs],
        compiler_params=pltpu.CompilerParams(vmem_limit_bytes=50 * 1024 * 1024),
        cost_estimate=pl.CostEstimate(
            flops=flops * slots * heads_dev * seq_dev * key_count * HEAD_DIM * 2,
            bytes_accessed=8 * 1024 * 1024,
            transcendentals=slots * heads_dev * seq_dev * key_count,
        ),
    )(scalars, *rows, keys, key_pos)


def on_device(
    block_in,
    lengths,
    out_cot,
    ln1_gain,
    ln1_bias,
    w_q,
    b_q,
    w_kv,
    b_v,
    w_out,
    b_out,
    ln2_gain,
    ln2_bias,
    w_up,
    b_up,
    w_down,
    b_down,
):
    blk_count = lax.axis_size("blk")
    blk = lax.axis_index("blk")
    head = lax.axis_index("head")
    z_count = blk_count // 2
    z, x = blk // 2, blk % 2
    y, core = head // 2, head % 2
    slots = lax.axis_size("head")
    seq_dev = block_in.shape[1]
    width = block_in.shape[2]
    depth = w_q.shape[0]
    q_dev = w_q.shape[1]
    ff_dev = w_up.shape[1]
    unit = ff_dev // 2
    part_unit = unit // 2
    plane = [(1, 0), (0, 2), (1, 2)]
    z_groups = [[2 * i + j for i in range(z_count)] for j in range(2)]

    def gather_z(values):
        return lax.all_gather(values, "blk", axis=0, axis_index_groups=z_groups)

    def scatter_z(values):
        return lax.psum_scatter(
            values, "blk", scatter_dimension=0, axis_index_groups=z_groups
        )

    def gather_head(values):
        pair = jnp.stack([values, flip(values, head_bits=2)])
        other = flip(pair, head_bits=1)
        return jnp.stack([pair, other], axis=1).reshape((slots,) + values.shape)

    def head_core(values):
        parts = values.reshape((2, 2) + values.shape[1:])
        return wide(parts[:, 0]) + wide(flip(low(parts[:, 1]), head_bits=1))

    def head_y(half):
        return half[0] + wide(flip(low(half[1]), head_bits=2))

    def scatter_head(values):
        return head_y(head_core(values))

    def gather_xy(values):
        return jnp.stack([values] + [flip(values, *bits) for bits in plane])

    def gather_core(mine):
        return jnp.concatenate([mine, flip(mine, head_bits=1)]).reshape(-1, width)

    def plane_core(values):
        parts = values.reshape((2, 4, seq_dev, width))
        return parts[0] + wide(flip(low(parts[1]), head_bits=1))

    def plane_xy(half):
        total = half[0]
        for i, bits in enumerate(plane):
            total = total + wide(flip(low(half[i + 1]), *bits))
        return total

    def swap_units(weights):
        own = lax.dynamic_slice_in_dim(weights, x * unit, unit, 1)
        other = lax.dynamic_slice_in_dim(weights, (1 - x) * unit, unit, 1)
        return in_order(own, flip(other, blk_bits=1), x, 0).reshape(2 * depth, unit)

    def gather_x(mine):
        return in_order(mine, flip(mine, blk_bits=1), x, 1).reshape(width, -1)

    mine = gather_z(jnp.concatenate([w_q, w_out]))
    mine_q, mine_out = mine[:, :depth], mine[:, depth:]
    full_q = gather_x(mine_q)
    def gather_units(weights):
        mine = swap_units(weights)
        return [
            gather_z(mine[:, i * part_unit : (i + 1) * part_unit]).reshape(width, part_unit)
            for i in range(2)
        ]

    full_up = gather_units(w_up)
    full_down = gather_units(w_down)

    own_rows = wide(block_in[0])
    positions = jnp.arange(seq_dev, dtype=jnp.int32)
    own_valid = blk * seq_dev + positions < lengths[head]
    attn_in = layer_norm(own_rows, ln1_gain, ln1_bias).astype(LOW)
    value_bias = jnp.concatenate([jnp.zeros((HEAD_DIM,), jnp.float32), b_v])
    keys = (plain_dot(attn_in, w_kv) + value_bias).astype(LOW)[None]
    bit = blk_count // 2
    while bit:
        keys = jnp.stack([keys, flip(keys, blk_bits=bit)], axis=1)
        keys = keys.reshape((-1,) + keys.shape[2:])
        bit //= 2
    keys = gather_head(keys).reshape(slots, blk_count * seq_dev, 2 * HEAD_DIM)
    key_blocks = blk ^ jnp.arange(blk_count, dtype=jnp.int32)
    key_pos = (key_blocks[:, None] * seq_dev + positions[None, :]).reshape(1, -1)
    slot_ids = head ^ jnp.arange(slots, dtype=jnp.int32)
    scalars = jnp.concatenate([(blk * seq_dev)[None], lengths[slot_ids]]).astype(jnp.int32)
    group_in = gather_head(attn_in).reshape(slots * seq_dev, width)

    own_cot = jnp.where(own_valid[:, None], out_cot[0], jnp.zeros_like(out_cot[0]))
    cot_rows = gather_core(gather_xy(own_cot))
    own_cot = wide(own_cot)

    column_start = head * q_dev
    query_bias = lax.dynamic_slice_in_dim(b_q, column_start, q_dev)
    queries = (plain_dot(group_in, full_q) + query_bias).astype(LOW)
    queries, mine_out = tie(queries, mine_out)
    full_out = gather_x(mine_out)
    (attn_low,) = attention_call(
        forward_kernel, ("row",), scalars, (queries,), keys, key_pos, seq_dev, 2
    )
    attn_low, full_up[0] = tie(attn_low, full_up[0])
    attn_part = col_dot(attn_low, full_out).reshape(slots, seq_dev, width)
    hidden_res = own_rows + scatter_head(attn_part) + b_out

    hidden_res, full_up[1] = tie(hidden_res, full_up[1])
    normed_two = layer_norm(hidden_res, ln2_gain, ln2_bias).astype(LOW)
    mine_in, full_down[0] = tie(gather_xy(normed_two), full_down[0])
    ffn_in = gather_core(mine_in)
    unit_start = head * ff_dev + x * unit

    def gelu(i):
        bias = lax.dynamic_slice_in_dim(b_up, unit_start + i * part_unit, part_unit)
        value, pull = jax.vjp(
            partial(jax.nn.gelu, approximate=True), plain_dot(ffn_in, full_up[i]) + bias
        )
        return low(value), pull

    def scatter_units(grads):
        return scatter_z(grads.reshape(z_count, 2 * depth, part_unit))

    activated, gelu_pulls = zip(*[gelu(i) for i in range(2)])
    activated = tie(*activated)
    grad_down = [low(row_dot(cot_rows, v)) for v in activated]
    *grad_down, full_down[1] = tie(*grad_down, full_down[1])
    sums_down = [scatter_units(v) for v in grad_down]
    grad_up_rows = [
        low(gelu_pulls[i](plain_dot(cot_rows, full_down[i]))[0]) for i in range(2)
    ]
    ffn_in_grad = plane_core(sum(col_dot(grad_up_rows[i], full_up[i]) for i in range(2)))
    ffn_in_grad = plane_xy(ffn_in_grad)
    ffn_part = plane_core(sum(col_dot(activated[i], full_down[i]) for i in range(2)))
    grad_up = [low(row_dot(ffn_in, v)) for v in grad_up_rows]
    ffn_in_grad, ffn_part, sums_down[0], *grad_up = tie(
        ffn_in_grad, ffn_part, sums_down[0], *grad_up
    )
    sums_up = [scatter_units(v) for v in grad_up]
    grad_up_bias = jnp.concatenate(
        [jnp.sum(v, axis=0, dtype=jnp.float32) for v in grad_up_rows]
    )

    norm_two_value, norm_two_pull = jax.vjp(layer_norm, hidden_res, ln2_gain, ln2_bias)
    res_grad, grad_ln2_gain, grad_ln2_bias = norm_two_pull(ffn_in_grad)
    res_total = own_cot + res_grad

    cot_attn = gather_head(res_total.astype(LOW)).reshape(slots * seq_dev, width)
    cot_attn, sums_down[1], ffn_part = tie(cot_attn, sums_down[1], ffn_part)
    output = low(hidden_res + plane_xy(ffn_part) + b_down)[None]
    attn_grad = plain_dot(cot_attn, full_out).astype(LOW)
    query_low, kv_grad = attention_call(
        backward_kernel,
        ("row", "key"),
        scalars,
        (queries, attn_grad),
        keys,
        key_pos,
        seq_dev,
        5,
    )
    query_low, kv_grad, output = tie(query_low, kv_grad, output)
    half_kv = head_core(kv_grad.reshape(slots, blk_count, seq_dev, 2 * HEAD_DIM))
    half_kv, cot_late, in_late = tie(half_kv, cot_attn, group_in)

    def sides(grads):
        parts = grads.reshape(z_count, 2, depth, q_dev)
        return take(parts, x, 1), low(take(parts, 1 - x, 1))

    grad_out, out_across = sides(row_dot(cot_late, attn_low))
    grad_q, q_across = sides(row_dot(in_late, query_low))
    out_across = flip(out_across, blk_bits=1)
    part, sums_up[0], grad_out, grad_q, q_across = tie(
        head_y(half_kv), sums_up[0], grad_out, grad_q, q_across
    )
    sum_out = wide(scatter_z(low(grad_out + wide(out_across))))
    bit = 1
    while bit < blk_count:
        pair = part.reshape((-1, 2) + part.shape[1:])
        part = pair[:, 0] + wide(flip(low(pair[:, 1]), blk_bits=bit))
        if bit == 1:
            part, q_across = tie(part, q_across)
            q_across = flip(q_across, blk_bits=1)
        bit *= 2
    own_kv_grad = low(part[0])
    sum_q = wide(scatter_z(low(grad_q + wide(q_across))))
    attn_in_grad = col_dot(query_low, full_q).reshape(slots, seq_dev, width)
    norm_one_grad = scatter_head(attn_in_grad) + col_dot(own_kv_grad, w_kv)
    norm_one_value, norm_one_pull = jax.vjp(layer_norm, own_rows, ln1_gain, ln1_bias)
    input_part, grad_ln1_gain, grad_ln1_bias = norm_one_pull(norm_one_grad)
    input_grad = res_total + input_part

    def ff_sum(sums):
        parts = jnp.concatenate(sums, axis=-1).reshape(2, depth, unit)
        own, other = take(parts, x, 0), flip(take(parts, 1 - x, 0), blk_bits=1)
        first = x == 0
        return wide(
            jnp.concatenate([jnp.where(first, own, other), jnp.where(first, other, own)], axis=-1)
        )

    sum_down = ff_sum(sums_down)

    grad_kv = row_dot(attn_in, own_kv_grad)
    grad_b_q = lax.dynamic_update_slice_in_dim(
        jnp.zeros((width,), jnp.float32),
        jnp.sum(query_low, axis=0, dtype=jnp.float32),
        column_start,
        0,
    )
    grad_b_up = lax.dynamic_update_slice_in_dim(jnp.zeros_like(b_up), grad_up_bias, unit_start, 0)
    grad_b_v = jnp.sum(own_kv_grad[:, HEAD_DIM:], axis=0, dtype=jnp.float32)
    lines = jnp.concatenate(
        [
            jnp.stack(
                [
                    grad_ln1_gain,
                    grad_ln1_bias,
                    grad_b_q,
                    jnp.sum(res_total, axis=0),
                    grad_ln2_gain,
                    grad_ln2_bias,
                    jnp.sum(own_cot, axis=0),
                    jnp.pad(grad_b_v, (0, width - HEAD_DIM)),
                ]
            ),
            grad_b_up.reshape(-1, width),
        ]
    ).reshape(-1, 2 * HEAD_DIM)
    line_count = lines.shape[0]

    def exchange(lines, rows, **bits):
        first = rounded(lines)
        second = rounded(lines - first)
        got = flip(jnp.concatenate([low(first), low(second), low(rows)]), **bits)
        lines = (first + second) + (wide(got[:line_count]) + wide(got[line_count : 2 * line_count]))
        return lines, wide(got[2 * line_count :])

    def halved(lines, rows, index, **bits):
        pair = rows.reshape((2, -1) + rows.shape[1:])
        lines, got = exchange(lines, take(pair, 1 - index, 0), **bits)
        return lines, take(pair, index, 0) + got

    def joined(values, index, **bits):
        whole = in_order(values, flip(values, **bits), index, 0)
        return whole.reshape((-1,) + values.shape[1:])

    lines, rows = halved(lines, grad_kv, core, head_bits=1)
    lines, rows = halved(lines, rows, x, blk_bits=1)
    rows, sums_up[1] = tie(rows, sums_up[1])
    sum_up = ff_sum(sums_up)
    lines, rows = halved(lines, rows, y, head_bits=2)
    bit = 2
    while bit < blk_count:
        lines, got = exchange(lines, rows, blk_bits=bit)
        rows = rounded(rows) + got
        bit *= 2
    rows = joined(low(rows), y, head_bits=2)
    rows = joined(rows, x, blk_bits=1)
    sum_kv = wide(joined(rows, core, head_bits=1))
    lines = lines.reshape(-1, width)
    (
        sum_ln1_gain,
        sum_ln1_bias,
        sum_q_bias,
        sum_out_bias,
        sum_ln2_gain,
        sum_ln2_bias,
        sum_down_bias,
        sum_v_bias,
    ) = lines[:8]
    sum_v_bias = sum_v_bias[:HEAD_DIM]
    sum_up_bias = lines[8:].reshape(-1)
    return (
        output,
        input_grad[None],
        sum_ln1_gain,
        sum_ln1_bias,
        sum_q,
        sum_q_bias,
        sum_kv,
        sum_v_bias,
        sum_out,
        sum_out_bias,
        sum_ln2_gain,
        sum_ln2_bias,
        sum_up,
        sum_up_bias,
        sum_down,
        sum_down_bias,
    )


def solution(mesh):
    rows = P("head", "blk", None)
    weights = P("blk", "head")
    in_specs = (
        rows,
        P(),
        rows,
        P(),
        P(),
        weights,
        P(),
        P(),
        P(),
        weights,
        P(),
        P(),
        P(),
        weights,
        P(),
        weights,
        P(),
    )
    out_specs = (
        rows,
        rows,
        P(),
        P(),
        weights,
        P(),
        P(),
        P(),
        weights,
        P(),
        P(),
        P(),
        weights,
        P(),
        weights,
        P(),
    )
    return jax.shard_map(
        on_device, mesh=mesh, in_specs=in_specs, out_specs=out_specs, check_vma=False
    )
```

```python
from functools import partial

import jax
import jax.numpy as jnp
from jax import lax
from jax.experimental import pallas as pl
from jax.experimental.pallas import tpu as pltpu
from jax.sharding import PartitionSpec as P

HEADS = 16
HEAD_DIM = 128
EPSILON = 1e-05
SCALE = HEAD_DIM ** (-0.5)
LOW = jnp.bfloat16


def layer_norm(values, gain, bias):
    center = values - jnp.mean(values, axis=-1, keepdims=True)
    spread = jnp.mean(center * center, axis=-1, keepdims=True)
    return center * lax.rsqrt(spread + EPSILON) * gain + bias


def plain_dot(left, right):
    return jnp.dot(left, right, preferred_element_type=jnp.float32)


def row_dot(left, right):
    return lax.dot_general(
        left, right, (((0,), (0,)), ((), ())), preferred_element_type=jnp.float32
    )


def col_dot(left, right):
    return lax.dot_general(
        left, right, (((1,), (1,)), ((), ())), preferred_element_type=jnp.float32
    )


def wide(values):
    return values.astype(jnp.float32)


def low(values):
    return values.astype(LOW)


def rounded(values):
    return lax.reduce_precision(values, 8, 7)


def flip(values, blk_bits=0, head_bits=0):
    blk_count = lax.axis_size("blk")
    head_count = lax.axis_size("head")
    pairs = [
        (b * head_count + h, (b ^ blk_bits) * head_count + (h ^ head_bits))
        for b in range(blk_count)
        for h in range(head_count)
    ]
    return lax.ppermute(values, ("blk", "head"), pairs)


def in_order(own, other, index, axis):
    first = index == 0
    return jnp.stack([jnp.where(first, own, other), jnp.where(first, other, own)], axis=axis)


def tie(*values):
    return lax.optimization_barrier(values)


def take(values, index, axis):
    return lax.dynamic_index_in_dim(values, index, axis, keepdims=False)


def stacked(ref, heads):
    return jnp.concatenate(
        [ref[:, h * HEAD_DIM : (h + 1) * HEAD_DIM] for h in range(heads)], axis=0
    )


def probabilities(query, key, key_pos, start, length, seq_dev):
    raw = col_dot(query, key) * SCALE
    row = lax.broadcasted_iota(jnp.int32, (query.shape[0], 1), 0)
    row_pos = start + row % seq_dev
    limit = jnp.minimum(row_pos, length - 1)
    masked = jnp.where(key_pos <= limit, raw, -1e30)
    weights = jnp.exp(masked - jnp.max(masked, axis=-1, keepdims=True))
    return weights * (1.0 / jnp.sum(weights, axis=-1, keepdims=True))


def forward_kernel(heads, scalars, q_ref, kv_ref, pos_ref, o_ref):
    seq_dev = q_ref.shape[0]
    key = kv_ref[0, :, :HEAD_DIM]
    value = kv_ref[0, :, HEAD_DIM:]
    prob = probabilities(
        stacked(q_ref, heads),
        key,
        pos_ref[...],
        scalars[0],
        scalars[1 + pl.program_id(0)],
        seq_dev,
    )
    out = plain_dot(prob.astype(LOW), value).astype(LOW)
    for h in range(heads):
        o_ref[:, h * HEAD_DIM : (h + 1) * HEAD_DIM] = out[h * seq_dev : (h + 1) * seq_dev]


def backward_kernel(heads, scalars, q_ref, go_ref, kv_ref, pos_ref, gq_ref, gkv_ref):
    seq_dev = q_ref.shape[0]
    key = kv_ref[0, :, :HEAD_DIM]
    value = kv_ref[0, :, HEAD_DIM:]
    query = stacked(q_ref, heads)
    grad = stacked(go_ref, heads)
    prob = probabilities(
        query,
        key,
        pos_ref[...],
        scalars[0],
        scalars[1 + pl.program_id(0)],
        seq_dev,
    )
    prob_low = prob.astype(LOW)
    prob_grad = col_dot(grad, value)
    delta = jnp.sum(wide(prob_low) * prob_grad, axis=-1, keepdims=True)
    score_grad = (prob * (prob_grad - delta)).astype(LOW)
    out = (plain_dot(score_grad, key) * SCALE).astype(LOW)
    for h in range(heads):
        gq_ref[:, h * HEAD_DIM : (h + 1) * HEAD_DIM] = out[h * seq_dev : (h + 1) * seq_dev]
    key_grad = row_dot(score_grad, query) * SCALE
    value_grad = row_dot(prob_low, grad)

    @pl.when(pl.program_id(1) == 0)
    def _():
        gkv_ref[0, :, :HEAD_DIM] = key_grad
        gkv_ref[0, :, HEAD_DIM:] = value_grad

    @pl.when(pl.program_id(1) > 0)
    def _():
        gkv_ref[0, :, :HEAD_DIM] += key_grad
        gkv_ref[0, :, HEAD_DIM:] += value_grad


def attention_call(kernel, outs, scalars, rows, keys, key_pos, seq_dev, flops):
    slots, key_count, _ = keys.shape
    heads_dev = rows[0].shape[1] // HEAD_DIM
    heads = max(1, min(heads_dev, heads_dev * 1024 // key_count))
    row_spec = pl.BlockSpec((seq_dev, heads * HEAD_DIM), lambda s, g, *_: (s, g))
    key_spec = pl.BlockSpec((1, key_count, 2 * HEAD_DIM), lambda s, g, *_: (s, 0, 0))
    pos_spec = pl.BlockSpec((1, key_count), lambda s, g, *_: (0, 0))
    shapes = {
        "row": (jax.ShapeDtypeStruct(rows[0].shape, LOW), row_spec),
        "key": (jax.ShapeDtypeStruct(keys.shape, jnp.float32), key_spec),
    }
    return pl.pallas_call(
        partial(kernel, heads),
        grid_spec=pltpu.PrefetchScalarGridSpec(
            num_scalar_prefetch=1,
            grid=(slots, heads_dev // heads),
            in_specs=[row_spec] * len(rows) + [key_spec, pos_spec],
            out_specs=[shapes[o][1] for o in outs],
        ),
        out_shape=[shapes[o][0] for o in outs],
        compiler_params=pltpu.CompilerParams(vmem_limit_bytes=50 * 1024 * 1024),
        cost_estimate=pl.CostEstimate(
            flops=flops * slots * heads_dev * seq_dev * key_count * HEAD_DIM * 2,
            bytes_accessed=8 * 1024 * 1024,
            transcendentals=slots * heads_dev * seq_dev * key_count,
        ),
    )(scalars, *rows, keys, key_pos)


def on_device(
    block_in,
    lengths,
    out_cot,
    ln1_gain,
    ln1_bias,
    w_q,
    b_q,
    w_kv,
    b_v,
    w_out,
    b_out,
    ln2_gain,
    ln2_bias,
    w_up,
    b_up,
    w_down,
    b_down,
):
    blk_count = lax.axis_size("blk")
    blk = lax.axis_index("blk")
    head = lax.axis_index("head")
    z_count = blk_count // 2
    z, x = blk // 2, blk % 2
    y, core = head // 2, head % 2
    slots = lax.axis_size("head")
    seq_dev = block_in.shape[1]
    width = block_in.shape[2]
    depth = w_q.shape[0]
    q_dev = w_q.shape[1]
    ff_dev = w_up.shape[1]
    unit = ff_dev // 2
    part_unit = unit // 2
    plane = [(1, 0), (0, 2), (1, 2)]
    z_groups = [[2 * i + j for i in range(z_count)] for j in range(2)]

    def gather_z(values):
        return lax.all_gather(values, "blk", axis=0, axis_index_groups=z_groups)

    def scatter_z(values):
        return lax.psum_scatter(
            values, "blk", scatter_dimension=0, axis_index_groups=z_groups
        )

    def pair_y(values):
        return jnp.stack([values, flip(values, head_bits=2)])

    def pair_core(pair):
        return jnp.concatenate([pair, flip(pair, head_bits=1)])

    def gather_head(values):
        return pair_core(pair_y(values))

    def add_core(left, right):
        rows = left[0].shape[0] // 2
        send = sum(col_dot(v[rows:], w) for v, w in zip(left, right))
        keep = sum(col_dot(v[:rows], w) for v, w in zip(left, right))
        keep = keep + wide(flip(low(send), head_bits=1))
        return keep.reshape(-1, seq_dev, width)

    def add_y(half):
        return half[0] + wide(flip(low(half[1]), head_bits=2))

    def gather_xy(values):
        return jnp.stack([values] + [flip(values, *bits) for bits in plane])

    def gather_core(mine):
        return jnp.concatenate([mine, flip(mine, head_bits=1)]).reshape(-1, width)

    def plane_xy(half):
        total = half[0]
        for i, bits in enumerate(plane):
            total = total + wide(flip(low(half[i + 1]), *bits))
        return total

    def swap_units(weights):
        own = lax.dynamic_slice_in_dim(weights, x * unit, unit, 1)
        other = lax.dynamic_slice_in_dim(weights, (1 - x) * unit, unit, 1)
        return in_order(own, flip(other, blk_bits=1), x, 0).reshape(2 * depth, unit)

    def gather_x(mine):
        return in_order(mine, flip(mine, blk_bits=1), x, 1).reshape(width, -1)

    mine = gather_z(jnp.concatenate([w_q, w_out]))
    mine_q, mine_out = mine[:, :depth], mine[:, depth:]
    full_q = gather_x(mine_q)
    def gather_units(weights):
        mine = swap_units(weights)
        return [
            gather_z(mine[:, i * part_unit : (i + 1) * part_unit]).reshape(width, part_unit)
            for i in range(2)
        ]

    full_up = gather_units(w_up)
    full_down = gather_units(w_down)

    own_rows = wide(block_in[0])
    positions = jnp.arange(seq_dev, dtype=jnp.int32)
    own_valid = blk * seq_dev + positions < lengths[head]
    attn_in = layer_norm(own_rows, ln1_gain, ln1_bias).astype(LOW)
    value_bias = jnp.concatenate([jnp.zeros((HEAD_DIM,), jnp.float32), b_v])
    keys = (plain_dot(attn_in, w_kv) + value_bias).astype(LOW)[None]
    bit = blk_count // 2
    while bit:
        keys = jnp.stack([keys, flip(keys, blk_bits=bit)], axis=1)
        keys = keys.reshape((-1,) + keys.shape[2:])
        bit //= 2
    keys = gather_head(keys).reshape(slots, blk_count * seq_dev, 2 * HEAD_DIM)
    key_blocks = blk ^ jnp.arange(blk_count, dtype=jnp.int32)
    key_pos = (key_blocks[:, None] * seq_dev + positions[None, :]).reshape(1, -1)
    slot_ids = head ^ jnp.array([0, 2, 1, 3], jnp.int32)
    scalars = jnp.concatenate([(blk * seq_dev)[None], lengths[slot_ids]]).astype(jnp.int32)
    group_in = gather_head(attn_in).reshape(slots * seq_dev, width)

    own_cot = jnp.where(own_valid[:, None], out_cot[0], jnp.zeros_like(out_cot[0]))
    cot_rows = gather_core(gather_xy(own_cot))
    own_cot = wide(own_cot)

    column_start = head * q_dev
    query_bias = lax.dynamic_slice_in_dim(b_q, column_start, q_dev)
    queries = (plain_dot(group_in, full_q) + query_bias).astype(LOW)
    queries, mine_out = tie(queries, mine_out)
    full_out = gather_x(mine_out)
    (attn_low,) = attention_call(
        forward_kernel, ("row",), scalars, (queries,), keys, key_pos, seq_dev, 2
    )
    attn_low, full_up[0] = tie(attn_low, full_up[0])
    hidden_res = own_rows + add_y(add_core([attn_low], [full_out])) + b_out
    hidden_res, full_up[1], cot_rows = tie(hidden_res, full_up[1], cot_rows)
    normed_two = layer_norm(hidden_res, ln2_gain, ln2_bias).astype(LOW)
    mine_in, full_down[0] = tie(gather_xy(normed_two), full_down[0])
    ffn_in = gather_core(mine_in)
    unit_start = head * ff_dev + x * unit

    def gelu(i):
        bias = lax.dynamic_slice_in_dim(b_up, unit_start + i * part_unit, part_unit)
        value, pull = jax.vjp(
            partial(jax.nn.gelu, approximate=True), plain_dot(ffn_in, full_up[i]) + bias
        )
        return low(value), pull

    def scatter_units(grads):
        return scatter_z(grads.reshape(z_count, 2 * depth, part_unit))

    activated, gelu_pulls = zip(*[gelu(i) for i in range(2)])
    activated = tie(*activated)
    grad_down = [low(row_dot(cot_rows, v)) for v in activated]

    def back(i):
        return low(gelu_pulls[i](plain_dot(cot_rows, full_down[i]))[0])

    *grad_down, first_rows, full_down[1] = tie(*grad_down, back(0), full_down[1])
    sums_down = [scatter_units(grad_down[0])]
    grad_up_rows = [first_rows, back(1)]
    in_half = add_core(grad_up_rows, full_up)
    in_half, activated, grad_up_rows, grad_down = tie(
        in_half, activated, grad_up_rows, grad_down[1]
    )
    sums_down.append(scatter_units(grad_down))
    ffn_in_grad = plane_xy(in_half)
    grad_up = [low(row_dot(ffn_in, v)) for v in grad_up_rows]
    ffn_in_grad, sums_down[0], grad_up, activated = tie(
        ffn_in_grad, sums_down[0], grad_up, activated
    )
    ffn_half = add_core(activated, full_down)
    sums_up = [scatter_units(v) for v in grad_up]
    grad_up_bias = jnp.concatenate(
        [jnp.sum(v, axis=0, dtype=jnp.float32) for v in grad_up_rows]
    )

    norm_two_value, norm_two_pull = jax.vjp(layer_norm, hidden_res, ln2_gain, ln2_bias)
    res_grad, grad_ln2_gain, grad_ln2_bias = norm_two_pull(ffn_in_grad)
    res_total = own_cot + res_grad

    cot_pair, ffn_half = tie(pair_y(low(res_total)), ffn_half)
    cot_attn = pair_core(cot_pair).reshape(slots * seq_dev, width)
    cot_attn, sums_down[1] = tie(cot_attn, sums_down[1])
    attn_grad = plain_dot(cot_attn, full_out).astype(LOW)
    query_low, kv_grad = attention_call(
        backward_kernel,
        ("row", "key"),
        scalars,
        (queries, attn_grad),
        keys,
        key_pos,
        seq_dev,
        5,
    )
    kv_grad = kv_grad.reshape(slots, blk_count, seq_dev, 2 * HEAD_DIM)
    half_kv = kv_grad[:2] + wide(flip(low(kv_grad[2:]), head_bits=1))
    half_in = add_core([query_low], [full_q])
    half_kv, half_in, cot_late, in_late = tie(half_kv, half_in, cot_attn, group_in)

    def sides(grads):
        parts = grads.reshape(z_count, 2, depth, q_dev)
        return take(parts, x, 1), low(take(parts, 1 - x, 1))

    grad_q, q_across = sides(row_dot(in_late, query_low))
    q_across = flip(q_across, blk_bits=1)
    part, grad_q, cot_late, sums_up[0] = tie(add_y(half_kv), grad_q, cot_late, sums_up[0])
    grad_out, out_across = sides(row_dot(cot_late, attn_low))
    bit = 1
    while bit < blk_count:
        pair = part.reshape((-1, 2) + part.shape[1:])
        part = pair[:, 0] + wide(flip(low(pair[:, 1]), blk_bits=bit))
        if bit == 1:
            part, grad_out, out_across, q_across = tie(part, grad_out, out_across, q_across)
            sum_q = wide(scatter_z(low(grad_q + wide(q_across))))
            out_across = flip(out_across, blk_bits=1)
        bit *= 2
    own_kv_grad = low(part[0])
    norm_one_grad = add_y(half_in) + col_dot(own_kv_grad, w_kv)
    norm_one_value, norm_one_pull = jax.vjp(layer_norm, own_rows, ln1_gain, ln1_bias)
    input_part, grad_ln1_gain, grad_ln1_bias = norm_one_pull(norm_one_grad)
    input_grad = res_total + input_part

    def ff_sum(sums):
        parts = jnp.concatenate(sums, axis=-1).reshape(2, depth, unit)
        own, other = take(parts, x, 0), flip(take(parts, 1 - x, 0), blk_bits=1)
        first = x == 0
        return wide(
            jnp.concatenate([jnp.where(first, own, other), jnp.where(first, other, own)], axis=-1)
        )

    grad_kv, out_across = tie(row_dot(attn_in, own_kv_grad), out_across)
    out_total = low(grad_out + wide(out_across))
    grad_b_q = lax.dynamic_update_slice_in_dim(
        jnp.zeros((width,), jnp.float32),
        jnp.sum(query_low, axis=0, dtype=jnp.float32),
        column_start,
        0,
    )
    grad_b_up = lax.dynamic_update_slice_in_dim(jnp.zeros_like(b_up), grad_up_bias, unit_start, 0)
    grad_b_v = jnp.sum(own_kv_grad[:, HEAD_DIM:], axis=0, dtype=jnp.float32)
    lines = jnp.concatenate(
        [
            jnp.stack(
                [
                    grad_ln1_gain,
                    grad_ln1_bias,
                    grad_b_q,
                    jnp.sum(res_total, axis=0),
                    grad_ln2_gain,
                    grad_ln2_bias,
                    jnp.sum(own_cot, axis=0),
                    jnp.pad(grad_b_v, (0, width - HEAD_DIM)),
                ]
            ),
            grad_b_up.reshape(-1, width),
        ]
    ).reshape(-1, 2 * HEAD_DIM)
    line_count = lines.shape[0]

    def exchange(lines, rows, **bits):
        first = rounded(lines)
        second = rounded(lines - first)
        got = flip(jnp.concatenate([low(first), low(second), low(rows)]), **bits)
        lines = (first + second) + (wide(got[:line_count]) + wide(got[line_count : 2 * line_count]))
        return lines, wide(got[2 * line_count :])

    def halved(lines, rows, index, **bits):
        pair = rows.reshape((2, -1) + rows.shape[1:])
        lines, got = exchange(lines, take(pair, 1 - index, 0), **bits)
        return lines, take(pair, index, 0) + got

    def joined(values, index, **bits):
        whole = in_order(values, flip(values, **bits), index, 0)
        return whole.reshape((-1,) + values.shape[1:])

    lines, rows = halved(lines, grad_kv, core, head_bits=1)
    lines, rows = halved(lines, rows, x, blk_bits=1)
    rows, ffn_half = tie(rows, ffn_half)
    output = low(hidden_res + plane_xy(ffn_half) + b_down)[None]
    lines, rows = halved(lines, rows, y, head_bits=2)
    rows, sums_down = tie(rows, sums_down)
    sum_down = ff_sum(sums_down)
    bit = 2
    while bit < blk_count:
        lines, got = exchange(lines, rows, blk_bits=bit)
        rows = rounded(rows) + got
        if bit == 2:
            rows, sum_q, sums_up[1] = tie(rows, sum_q, sums_up[1])
            sum_up = ff_sum(sums_up)
        bit *= 2
    rows, out_total = tie(rows, out_total)
    sum_out = wide(scatter_z(out_total))
    rows = joined(low(rows), y, head_bits=2)
    rows = joined(rows, x, blk_bits=1)
    sum_kv = wide(joined(rows, core, head_bits=1))
    lines = lines.reshape(-1, width)
    (
        sum_ln1_gain,
        sum_ln1_bias,
        sum_q_bias,
        sum_out_bias,
        sum_ln2_gain,
        sum_ln2_bias,
        sum_down_bias,
        sum_v_bias,
    ) = lines[:8]
    sum_v_bias = sum_v_bias[:HEAD_DIM]
    sum_up_bias = lines[8:].reshape(-1)
    return (
        output,
        input_grad[None],
        sum_ln1_gain,
        sum_ln1_bias,
        sum_q,
        sum_q_bias,
        sum_kv,
        sum_v_bias,
        sum_out,
        sum_out_bias,
        sum_ln2_gain,
        sum_ln2_bias,
        sum_up,
        sum_up_bias,
        sum_down,
        sum_down_bias,
    )


def solution(mesh):
    rows = P("head", "blk", None)
    weights = P("blk", "head")
    in_specs = (
        rows,
        P(),
        rows,
        P(),
        P(),
        weights,
        P(),
        P(),
        P(),
        weights,
        P(),
        P(),
        P(),
        weights,
        P(),
        weights,
        P(),
    )
    out_specs = (
        rows,
        rows,
        P(),
        P(),
        weights,
        P(),
        P(),
        P(),
        weights,
        P(),
        P(),
        P(),
        weights,
        P(),
        weights,
        P(),
    )
    return jax.shard_map(
        on_device, mesh=mesh, in_specs=in_specs, out_specs=out_specs, check_vma=False
    )
```

```python
from functools import partial

import jax
import jax.numpy as jnp
from jax import lax
from jax.experimental import pallas as pl
from jax.experimental.pallas import tpu as pltpu
from jax.sharding import PartitionSpec as P

HEADS = 16
HEAD_DIM = 128
EPSILON = 1e-05
SCALE = HEAD_DIM ** (-0.5)
LOW = jnp.bfloat16


def layer_norm(values, gain, bias):
    center = values - jnp.mean(values, axis=-1, keepdims=True)
    spread = jnp.mean(center * center, axis=-1, keepdims=True)
    return center * lax.rsqrt(spread + EPSILON) * gain + bias


def plain_dot(left, right):
    return jnp.dot(left, right, preferred_element_type=jnp.float32)


def row_dot(left, right):
    return lax.dot_general(
        left, right, (((0,), (0,)), ((), ())), preferred_element_type=jnp.float32
    )


def col_dot(left, right):
    return lax.dot_general(
        left, right, (((1,), (1,)), ((), ())), preferred_element_type=jnp.float32
    )


def wide(values):
    return values.astype(jnp.float32)


def low(values):
    return values.astype(LOW)


def rounded(values):
    return lax.reduce_precision(values, 8, 7)


def flip(values, blk_bits=0, head_bits=0):
    blk_count = lax.axis_size("blk")
    head_count = lax.axis_size("head")
    pairs = [
        (b * head_count + h, (b ^ blk_bits) * head_count + (h ^ head_bits))
        for b in range(blk_count)
        for h in range(head_count)
    ]
    return lax.ppermute(values, ("blk", "head"), pairs)


def in_order(own, other, index, axis):
    first = index == 0
    return jnp.stack([jnp.where(first, own, other), jnp.where(first, other, own)], axis=axis)


def tie(*values):
    return lax.optimization_barrier(values)


def take(values, index, axis):
    return lax.dynamic_index_in_dim(values, index, axis, keepdims=False)


def stacked(ref, heads):
    return jnp.concatenate(
        [ref[:, h * HEAD_DIM : (h + 1) * HEAD_DIM] for h in range(heads)], axis=0
    )


def probabilities(query, key, key_pos, start, length, seq_dev):
    raw = col_dot(query, key) * SCALE
    row = lax.broadcasted_iota(jnp.int32, (query.shape[0], 1), 0)
    row_pos = start + row % seq_dev
    limit = jnp.minimum(row_pos, length - 1)
    masked = jnp.where(key_pos <= limit, raw, -1e30)
    weights = jnp.exp(masked - jnp.max(masked, axis=-1, keepdims=True))
    return weights * (1.0 / jnp.sum(weights, axis=-1, keepdims=True))


def forward_kernel(heads, scalars, q_ref, kv_ref, pos_ref, o_ref):
    seq_dev = q_ref.shape[0]
    key = kv_ref[0, :, :HEAD_DIM]
    value = kv_ref[0, :, HEAD_DIM:]
    prob = probabilities(
        stacked(q_ref, heads),
        key,
        pos_ref[...],
        scalars[0],
        scalars[1 + pl.program_id(0)],
        seq_dev,
    )
    out = plain_dot(prob.astype(LOW), value).astype(LOW)
    for h in range(heads):
        o_ref[:, h * HEAD_DIM : (h + 1) * HEAD_DIM] = out[h * seq_dev : (h + 1) * seq_dev]


def backward_kernel(heads, scalars, q_ref, go_ref, kv_ref, pos_ref, gq_ref, gkv_ref, total_ref):
    seq_dev = q_ref.shape[0]
    key = kv_ref[0, :, :HEAD_DIM]
    value = kv_ref[0, :, HEAD_DIM:]
    query = stacked(q_ref, heads)
    grad = stacked(go_ref, heads)
    prob = probabilities(
        query,
        key,
        pos_ref[...],
        scalars[0],
        scalars[1 + pl.program_id(0)],
        seq_dev,
    )
    prob_low = prob.astype(LOW)
    prob_grad = col_dot(grad, value)
    delta = jnp.sum(wide(prob_low) * prob_grad, axis=-1, keepdims=True)
    score_grad = (prob * (prob_grad - delta)).astype(LOW)
    out = (plain_dot(score_grad, key) * SCALE).astype(LOW)
    for h in range(heads):
        gq_ref[:, h * HEAD_DIM : (h + 1) * HEAD_DIM] = out[h * seq_dev : (h + 1) * seq_dev]
    key_grad = row_dot(score_grad, query) * SCALE
    value_grad = row_dot(prob_low, grad)
    last = pl.num_programs(1) - 1

    @pl.when(pl.program_id(1) > 0)
    def _():
        total_ref[:, :HEAD_DIM] += key_grad
        total_ref[:, HEAD_DIM:] += value_grad

    @pl.when(pl.program_id(1) == 0)
    def _():
        total_ref[:, :HEAD_DIM] = key_grad
        total_ref[:, HEAD_DIM:] = value_grad

    @pl.when(pl.program_id(1) == last)
    def _():
        gkv_ref[0] = total_ref[...].astype(LOW)


def attention_call(kernel, outs, scalars, rows, keys, key_pos, seq_dev, flops):
    slots, key_count, _ = keys.shape
    heads_dev = rows[0].shape[1] // HEAD_DIM
    heads = max(1, min(heads_dev, heads_dev * 1024 // key_count))
    row_spec = pl.BlockSpec((seq_dev, heads * HEAD_DIM), lambda s, g, *_: (s, g))
    key_spec = pl.BlockSpec((1, key_count, 2 * HEAD_DIM), lambda s, g, *_: (s, 0, 0))
    pos_spec = pl.BlockSpec((1, key_count), lambda s, g, *_: (0, 0))
    shapes = {
        "row": (jax.ShapeDtypeStruct(rows[0].shape, LOW), row_spec),
        "key": (jax.ShapeDtypeStruct(keys.shape, LOW), key_spec),
    }
    return pl.pallas_call(
        partial(kernel, heads),
        grid_spec=pltpu.PrefetchScalarGridSpec(
            num_scalar_prefetch=1,
            grid=(slots, heads_dev // heads),
            in_specs=[row_spec] * len(rows) + [key_spec, pos_spec],
            out_specs=[shapes[o][1] for o in outs],
            scratch_shapes=[pltpu.VMEM(keys.shape[1:], jnp.float32) for o in outs if o == "key"],
        ),
        out_shape=[shapes[o][0] for o in outs],
        compiler_params=pltpu.CompilerParams(vmem_limit_bytes=50 * 1024 * 1024),
        cost_estimate=pl.CostEstimate(
            flops=flops * slots * heads_dev * seq_dev * key_count * HEAD_DIM * 2,
            bytes_accessed=8 * 1024 * 1024,
            transcendentals=slots * heads_dev * seq_dev * key_count,
        ),
    )(scalars, *rows, keys, key_pos)


def at(index, count):
    return pl.ds(pl.multiple_of(index * count, count), count)


def put_lines(ref, start, lines):
    first = lines.astype(LOW)
    count = lines.shape[0]
    ref[start : start + count] = first
    ref[start + count : start + 2 * count] = (lines - wide(first)).astype(LOW)


def get_lines(ref, start):
    count = (ref.shape[0] - start) // 2
    return wide(ref[start : start + count]) + wide(ref[start + count : start + 2 * count])


def first_stage(where, in_ref, grad_ref, lines_ref, send_ref, keep_ref, total_ref):
    total_ref[...] = row_dot(in_ref[...], grad_ref[...])
    count = keep_ref.shape[0]
    send_ref[:count] = total_ref[at(1 - where[0], count)].astype(LOW)
    keep_ref[...] = total_ref[at(where[0], count)]
    put_lines(send_ref, count, lines_ref[...])


def plane_stage(where, got_ref, sent_ref, keep_ref, *rest):
    *sends, mine_ref, total_ref = rest
    count, part = keep_ref.shape[0], mine_ref.shape[0]
    total_ref[...] = keep_ref[...] + wide(got_ref[:count])
    lines = get_lines(sent_ref, count) + get_lines(got_ref, count)
    mine_ref[...] = total_ref[at(where[1], part)]
    for i, send in enumerate(sends):
        send[:part] = total_ref[at(where[2 + i], part)].astype(LOW)
        put_lines(send, part, lines)


def plane_sum(x_ref, y_ref, xy_ref, sent_ref, mine_ref, send_ref):
    part = mine_ref.shape[0]
    total = mine_ref[...] + wide(x_ref[:part]) + wide(y_ref[:part]) + wide(xy_ref[:part])
    send_ref[:part] = total.astype(LOW)
    lines = get_lines(sent_ref, part) + get_lines(x_ref, part)
    put_lines(send_ref, part, lines + (get_lines(y_ref, part) + get_lines(xy_ref, part)))


def pair_sum(part, got_ref, sent_ref, send_ref):
    send_ref[:part] = (wide(sent_ref[:part]) + wide(got_ref[:part])).astype(LOW)
    put_lines(send_ref, part, get_lines(sent_ref, part) + get_lines(got_ref, part))


def last_sum(part, got_ref, sent_ref, rows_ref, lines_ref):
    rows_ref[...] = (wide(sent_ref[:part]) + wide(got_ref[:part])).astype(LOW)
    lines_ref[...] = get_lines(sent_ref, part) + get_lines(got_ref, part)


def join_stage(first, where, *refs):
    *parts, whole_ref = refs
    for i, part in enumerate(parts):
        whole_ref[at(where[first + i], part.shape[0])] = part[...].astype(whole_ref.dtype)


def small_call(kernel, outs, *args, scratch=(), where=None):
    lead = [] if where is None else [where]
    specs = [pl.BlockSpec(memory_space=pltpu.SMEM)] * len(lead)
    return pl.pallas_call(
        kernel,
        in_specs=specs + [pl.BlockSpec(memory_space=pltpu.VMEM)] * len(args),
        out_specs=[pl.BlockSpec(memory_space=pltpu.VMEM)] * len(outs),
        out_shape=[jax.ShapeDtypeStruct(*o) for o in outs],
        scratch_shapes=[pltpu.VMEM(*v) for v in scratch],
        compiler_params=pltpu.CompilerParams(vmem_limit_bytes=24 * 1024 * 1024),
        cost_estimate=pl.CostEstimate(
            flops=1024 * 1024, bytes_accessed=2 * 1024 * 1024, transcendentals=0
        ),
    )(*lead, *args)


def on_device(
    block_in,
    lengths,
    out_cot,
    ln1_gain,
    ln1_bias,
    w_q,
    b_q,
    w_kv,
    b_v,
    w_out,
    b_out,
    ln2_gain,
    ln2_bias,
    w_up,
    b_up,
    w_down,
    b_down,
):
    blk_count = lax.axis_size("blk")
    blk = lax.axis_index("blk")
    head = lax.axis_index("head")
    z_count = blk_count // 2
    z, x = blk // 2, blk % 2
    y, core = head // 2, head % 2
    slots = lax.axis_size("head")
    seq_dev = block_in.shape[1]
    width = block_in.shape[2]
    depth = w_q.shape[0]
    q_dev = w_q.shape[1]
    ff_dev = w_up.shape[1]
    unit = ff_dev // 2
    part_unit = unit // 2
    plane = [(0, 2), (1, 0), (1, 2)]
    z_groups = [[2 * i + j for i in range(z_count)] for j in range(2)]

    def gather_z(values):
        return lax.all_gather(values, "blk", axis=0, axis_index_groups=z_groups)

    def scatter_z(values):
        return lax.psum_scatter(
            values, "blk", scatter_dimension=0, axis_index_groups=z_groups
        )

    def pair_y(values):
        return jnp.stack([values, flip(values, head_bits=2)])

    def pair_core(pair):
        return jnp.concatenate([pair, flip(pair, head_bits=1)])

    def gather_head(values):
        return pair_core(pair_y(values))

    def add_core(left, right):
        rows = left[0].shape[0] // 2
        send = sum(col_dot(v[rows:], w) for v, w in zip(left, right))
        keep = sum(col_dot(v[:rows], w) for v, w in zip(left, right))
        keep = keep + wide(flip(low(send), head_bits=1))
        return keep.reshape(-1, seq_dev, width)

    def add_y(half):
        return half[0] + wide(flip(low(half[1]), head_bits=2))

    def gather_xy(values):
        return jnp.stack([values] + [flip(values, *bits) for bits in plane])

    def gather_core(mine):
        return jnp.concatenate([mine, flip(mine, head_bits=1)]).reshape(-1, width)

    def plane_xy(half):
        total = half[0]
        for i, bits in enumerate(plane):
            total = total + wide(flip(low(half[i + 1]), *bits))
        return total

    def swap_units(weights):
        own = lax.dynamic_slice_in_dim(weights, x * unit, unit, 1)
        other = lax.dynamic_slice_in_dim(weights, (1 - x) * unit, unit, 1)
        return in_order(own, flip(other, blk_bits=1), x, 0).reshape(2 * depth, unit)

    def gather_x(mine):
        return in_order(mine, flip(mine, blk_bits=1), x, 1).reshape(width, -1)

    mine = gather_z(jnp.concatenate([w_q, w_out]))
    mine_q, mine_out = mine[:, :depth], mine[:, depth:]
    full_q = gather_x(mine_q)
    def gather_units(mine):
        return [
            gather_z(mine[:, i * part_unit : (i + 1) * part_unit]).reshape(width, part_unit)
            for i in range(2)
        ]

    full_up = gather_units(swap_units(w_up))
    mine_down = swap_units(w_down)

    own_rows = wide(block_in[0])
    positions = jnp.arange(seq_dev, dtype=jnp.int32)
    own_valid = blk * seq_dev + positions < lengths[head]
    attn_in = layer_norm(own_rows, ln1_gain, ln1_bias).astype(LOW)
    value_bias = jnp.concatenate([jnp.zeros((HEAD_DIM,), jnp.float32), b_v])
    keys = (plain_dot(attn_in, w_kv) + value_bias).astype(LOW)[None]
    bit = blk_count // 2
    while bit:
        keys = jnp.stack([keys, flip(keys, blk_bits=bit)], axis=1)
        keys = keys.reshape((-1,) + keys.shape[2:])
        bit //= 2
    keys, mine_down = tie(keys, mine_down)
    full_down = gather_z(mine_down).reshape(width, unit)
    keys = gather_head(keys).reshape(slots, blk_count * seq_dev, 2 * HEAD_DIM)
    key_blocks = blk ^ jnp.arange(blk_count, dtype=jnp.int32)
    key_pos = (key_blocks[:, None] * seq_dev + positions[None, :]).reshape(1, -1)
    slot_ids = head ^ jnp.array([0, 2, 1, 3], jnp.int32)
    scalars = jnp.concatenate([(blk * seq_dev)[None], lengths[slot_ids]]).astype(jnp.int32)
    group_in = gather_head(attn_in).reshape(slots * seq_dev, width)

    own_cot = jnp.where(own_valid[:, None], out_cot[0], jnp.zeros_like(out_cot[0]))
    cot_mine = pair_y(own_cot)
    own_cot = wide(own_cot)

    column_start = head * q_dev
    query_bias = lax.dynamic_slice_in_dim(b_q, column_start, q_dev)
    queries = (plain_dot(group_in, full_q) + query_bias).astype(LOW)
    queries, mine_out, cot_mine = tie(queries, mine_out, cot_mine)
    full_out = gather_x(mine_out)
    (attn_low,) = attention_call(
        forward_kernel, ("row",), scalars, (queries,), keys, key_pos, seq_dev, 2
    )
    attn_low, full_up[0], cot_mine = tie(attn_low, full_up[0], cot_mine)
    cot_rows = gather_core(jnp.concatenate([cot_mine, flip(cot_mine, blk_bits=1)]))
    hidden_res = own_rows + add_y(add_core([attn_low], [full_out])) + b_out
    hidden_res, full_up[1], cot_rows = tie(hidden_res, full_up[1], cot_rows)
    normed_two = layer_norm(hidden_res, ln2_gain, ln2_bias).astype(LOW)
    ffn_in = gather_core(gather_xy(normed_two))
    unit_start = head * ff_dev + x * unit

    def gelu(i):
        bias = lax.dynamic_slice_in_dim(b_up, unit_start + i * part_unit, part_unit)
        value, pull = jax.vjp(
            partial(jax.nn.gelu, approximate=True), plain_dot(ffn_in, full_up[i]) + bias
        )
        return low(value), pull

    def scatter_units(grads):
        return scatter_z(grads.reshape(z_count, 2 * depth, part_unit))

    activated, gelu_pulls = zip(*[gelu(i) for i in range(2)])
    activated = tie(*activated)
    grad_down = [low(row_dot(cot_rows, v)) for v in activated]

    *grad_down, full_down = tie(*grad_down, full_down)
    sums_down = [scatter_units(grad_down[0])]
    grad_act = plain_dot(cot_rows, full_down)
    grad_up_rows = [
        low(gelu_pulls[i](grad_act[:, i * part_unit : (i + 1) * part_unit])[0]) for i in range(2)
    ]
    in_half = add_core(grad_up_rows, full_up)
    in_half, activated, grad_up_rows, grad_down = tie(
        in_half, activated, grad_up_rows, grad_down[1]
    )
    sums_down.append(scatter_units(grad_down))
    ffn_in_grad = plane_xy(in_half)
    grad_up = [low(row_dot(ffn_in, v)) for v in grad_up_rows]
    ffn_in_grad, sums_down[0], grad_up, activated = tie(
        ffn_in_grad, sums_down[0], grad_up, activated
    )
    ffn_half = add_core([jnp.concatenate(activated, axis=-1)], [full_down])
    sums_up = [scatter_units(v) for v in grad_up]
    grad_up_bias = jnp.concatenate(
        [jnp.sum(v, axis=0, dtype=jnp.float32) for v in grad_up_rows]
    )

    norm_two_value, norm_two_pull = jax.vjp(layer_norm, hidden_res, ln2_gain, ln2_bias)
    res_grad, grad_ln2_gain, grad_ln2_bias = norm_two_pull(ffn_in_grad)
    res_total = own_cot + res_grad

    cot_pair, ffn_half = tie(pair_y(low(res_total)), ffn_half)
    cot_attn = pair_core(cot_pair).reshape(slots * seq_dev, width)
    cot_attn, sums_down[1] = tie(cot_attn, sums_down[1])
    attn_grad = plain_dot(cot_attn, full_out).astype(LOW)
    query_low, kv_grad = attention_call(
        backward_kernel,
        ("row", "key"),
        scalars,
        (queries, attn_grad),
        keys,
        key_pos,
        seq_dev,
        5,
    )
    kv_grad = kv_grad.reshape(slots, blk_count, seq_dev, 2 * HEAD_DIM)
    half_kv = wide(kv_grad[:2]) + wide(flip(kv_grad[2:], head_bits=1))
    half_kv, query_low, cot_late, in_late = tie(half_kv, query_low, cot_attn, group_in)
    half_in = add_core([query_low], [full_q])

    def sides(grads):
        parts = grads.reshape(z_count, 2, depth, q_dev)
        return take(parts, x, 1), low(take(parts, 1 - x, 1))

    grad_q, q_across = sides(row_dot(in_late, query_low))
    q_across = flip(q_across, blk_bits=1)
    part, half_in, grad_q, cot_late, sums_up[0] = tie(
        add_y(half_kv), half_in, grad_q, cot_late, sums_up[0]
    )
    grad_out, out_across = sides(row_dot(cot_late, attn_low))
    bit = 1
    while bit < blk_count:
        pair = part.reshape((-1, 2) + part.shape[1:])
        part = pair[:, 0] + wide(flip(low(pair[:, 1]), blk_bits=bit))
        if bit == 1:
            part, grad_out, out_across, q_across = tie(part, grad_out, out_across, q_across)
            sum_q = wide(scatter_z(low(grad_q + wide(q_across))))
            out_across = flip(out_across, blk_bits=1)
        bit *= 2
    own_kv_grad = low(part[0])
    norm_one_grad = add_y(half_in) + col_dot(own_kv_grad, w_kv)
    norm_one_value, norm_one_pull = jax.vjp(layer_norm, own_rows, ln1_gain, ln1_bias)
    input_part, grad_ln1_gain, grad_ln1_bias = norm_one_pull(norm_one_grad)
    input_grad = res_total + input_part

    def ff_sum(sums):
        parts = jnp.concatenate(sums, axis=-1).reshape(2, depth, unit)
        own, other = take(parts, x, 0), flip(take(parts, 1 - x, 0), blk_bits=1)
        first = x == 0
        return wide(
            jnp.concatenate([jnp.where(first, own, other), jnp.where(first, other, own)], axis=-1)
        )

    grad_b_q = lax.dynamic_update_slice_in_dim(
        jnp.zeros((width,), jnp.float32),
        jnp.sum(query_low, axis=0, dtype=jnp.float32),
        column_start,
        0,
    )
    grad_b_up = lax.dynamic_update_slice_in_dim(jnp.zeros_like(b_up), grad_up_bias, unit_start, 0)
    grad_b_v = jnp.sum(own_kv_grad[:, HEAD_DIM:], axis=0, dtype=jnp.float32)
    lines = jnp.concatenate(
        [
            jnp.stack(
                [
                    grad_ln1_gain,
                    grad_ln1_bias,
                    grad_b_q,
                    jnp.sum(res_total, axis=0),
                    grad_ln2_gain,
                    grad_ln2_bias,
                    jnp.sum(own_cot, axis=0),
                    jnp.pad(grad_b_v, (0, width - HEAD_DIM)),
                ]
            ),
            grad_b_up.reshape(-1, width),
        ]
    ).reshape(-1, 2 * HEAD_DIM)
    line_count = lines.shape[0]

    columns = 2 * HEAD_DIM
    rows_half, rows_part = width // 2, width // 8
    message = (rows_part + 2 * line_count, columns)
    where = jnp.stack(
        [core, 2 * x + y, 2 * x + 1 - y, 2 * (1 - x) + y, 2 * (1 - x) + 1 - y, core, 1 - core]
    ).astype(jnp.int32)
    sent, keep = small_call(
        first_stage,
        [((rows_half + 2 * line_count, columns), LOW), ((rows_half, columns), jnp.float32)],
        attn_in,
        own_kv_grad,
        lines,
        scratch=[((width, columns), jnp.float32)],
        where=where,
    )
    *sent, keep = small_call(
        plane_stage,
        [(message, LOW)] * 3 + [((rows_part, columns), jnp.float32)],
        flip(sent, head_bits=1),
        sent,
        keep,
        scratch=[((rows_half, columns), jnp.float32)],
        where=where,
    )
    got = [flip(v, *bits) for v, bits in zip(sent, plane)]
    (sent,) = small_call(plane_sum, [(message, LOW)], *got, sent[0], keep)
    sent, ffn_half, sums_down, out_across = tie(sent, ffn_half, sums_down, out_across)
    sum_out = wide(scatter_z(low(grad_out + wide(out_across))))
    output = low(hidden_res + plane_xy(ffn_half) + b_down)[None]
    sum_down = ff_sum(sums_down)
    bit = 2
    while 2 * bit < blk_count:
        (sent,) = small_call(
            partial(pair_sum, rows_part), [(message, LOW)], flip(sent, blk_bits=bit), sent
        )
        bit *= 2
    rows, lines = small_call(
        partial(last_sum, rows_part),
        [((rows_part, columns), LOW), ((line_count, columns), jnp.float32)],
        flip(sent, blk_bits=bit),
        sent,
    )
    rows, sum_q, sums_up[1] = tie(rows, sum_q, sums_up[1])
    sum_up = ff_sum(sums_up)
    (rows,) = small_call(
        partial(join_stage, 1),
        [((rows_half, columns), LOW)],
        rows,
        *[flip(rows, *bits) for bits in plane],
        where=where,
    )
    (sum_kv,) = small_call(
        partial(join_stage, 5),
        [((width, columns), jnp.float32)],
        rows,
        flip(rows, head_bits=1),
        where=where,
    )
    lines = lines.reshape(-1, width)
    (
        sum_ln1_gain,
        sum_ln1_bias,
        sum_q_bias,
        sum_out_bias,
        sum_ln2_gain,
        sum_ln2_bias,
        sum_down_bias,
        sum_v_bias,
    ) = lines[:8]
    sum_v_bias = sum_v_bias[:HEAD_DIM]
    sum_up_bias = lines[8:].reshape(-1)
    return (
        output,
        input_grad[None],
        sum_ln1_gain,
        sum_ln1_bias,
        sum_q,
        sum_q_bias,
        sum_kv,
        sum_v_bias,
        sum_out,
        sum_out_bias,
        sum_ln2_gain,
        sum_ln2_bias,
        sum_up,
        sum_up_bias,
        sum_down,
        sum_down_bias,
    )


def solution(mesh):
    rows = P("head", "blk", None)
    weights = P("blk", "head")
    in_specs = (
        rows,
        P(),
        rows,
        P(),
        P(),
        weights,
        P(),
        P(),
        P(),
        weights,
        P(),
        P(),
        P(),
        weights,
        P(),
        weights,
        P(),
    )
    out_specs = (
        rows,
        rows,
        P(),
        P(),
        weights,
        P(),
        P(),
        P(),
        weights,
        P(),
        P(),
        P(),
        weights,
        P(),
        weights,
        P(),
    )
    return jax.shard_map(
        on_device, mesh=mesh, in_specs=in_specs, out_specs=out_specs, check_vma=False
    )
```

```python
from functools import partial

import jax
import jax.numpy as jnp
from jax import lax
from jax.experimental import pallas as pl
from jax.experimental.pallas import tpu as pltpu
from jax.sharding import PartitionSpec as P

HEADS = 16
HEAD_DIM = 128
EPSILON = 1e-05
SCALE = HEAD_DIM ** (-0.5)
LOW = jnp.bfloat16


def layer_norm(values, gain, bias):
    center = values - jnp.mean(values, axis=-1, keepdims=True)
    spread = jnp.mean(center * center, axis=-1, keepdims=True)
    return center * lax.rsqrt(spread + EPSILON) * gain + bias


def plain_dot(left, right):
    return jnp.dot(left, right, preferred_element_type=jnp.float32)


def row_dot(left, right):
    return lax.dot_general(
        left, right, (((0,), (0,)), ((), ())), preferred_element_type=jnp.float32
    )


def col_dot(left, right):
    return lax.dot_general(
        left, right, (((1,), (1,)), ((), ())), preferred_element_type=jnp.float32
    )


def wide(values):
    return values.astype(jnp.float32)


def low(values):
    return values.astype(LOW)


def rounded(values):
    return lax.reduce_precision(values, 8, 7)


def flip(values, blk_bits=0, head_bits=0):
    blk_count = lax.axis_size("blk")
    head_count = lax.axis_size("head")
    pairs = [
        (b * head_count + h, (b ^ blk_bits) * head_count + (h ^ head_bits))
        for b in range(blk_count)
        for h in range(head_count)
    ]
    return lax.ppermute(values, ("blk", "head"), pairs)


def in_order(own, other, index, axis):
    first = index == 0
    return jnp.stack([jnp.where(first, own, other), jnp.where(first, other, own)], axis=axis)


def tie(*values):
    return lax.optimization_barrier(values)


def take(values, index, axis):
    return lax.dynamic_index_in_dim(values, index, axis, keepdims=False)


def stacked(ref, heads):
    return jnp.concatenate(
        [ref[:, h * HEAD_DIM : (h + 1) * HEAD_DIM] for h in range(heads)], axis=0
    )


def probabilities(query, key, key_pos, start, length, seq_dev):
    raw = col_dot(query, key) * SCALE
    row = lax.broadcasted_iota(jnp.int32, (query.shape[0], 1), 0)
    row_pos = start + row % seq_dev
    limit = jnp.minimum(row_pos, length - 1)
    masked = jnp.where(key_pos <= limit, raw, -1e30)
    weights = jnp.exp(masked - jnp.max(masked, axis=-1, keepdims=True))
    return weights * (1.0 / jnp.sum(weights, axis=-1, keepdims=True))


def forward_kernel(heads, scalars, q_ref, kv_ref, pos_ref, o_ref):
    seq_dev = q_ref.shape[0]
    key = kv_ref[0, :, :HEAD_DIM]
    value = kv_ref[0, :, HEAD_DIM:]
    prob = probabilities(
        stacked(q_ref, heads),
        key,
        pos_ref[...],
        scalars[0],
        scalars[1 + pl.program_id(0)],
        seq_dev,
    )
    out = plain_dot(prob.astype(LOW), value).astype(LOW)
    for h in range(heads):
        o_ref[:, h * HEAD_DIM : (h + 1) * HEAD_DIM] = out[h * seq_dev : (h + 1) * seq_dev]


def backward_kernel(heads, scalars, q_ref, go_ref, kv_ref, pos_ref, gq_ref, gkv_ref, total_ref):
    seq_dev = q_ref.shape[0]
    key = kv_ref[0, :, :HEAD_DIM]
    value = kv_ref[0, :, HEAD_DIM:]
    query = stacked(q_ref, heads)
    grad = stacked(go_ref, heads)
    prob = probabilities(
        query,
        key,
        pos_ref[...],
        scalars[0],
        scalars[1 + pl.program_id(0)],
        seq_dev,
    )
    prob_low = prob.astype(LOW)
    prob_grad = col_dot(grad, value)
    delta = jnp.sum(wide(prob_low) * prob_grad, axis=-1, keepdims=True)
    score_grad = (prob * (prob_grad - delta)).astype(LOW)
    out = (plain_dot(score_grad, key) * SCALE).astype(LOW)
    for h in range(heads):
        gq_ref[:, h * HEAD_DIM : (h + 1) * HEAD_DIM] = out[h * seq_dev : (h + 1) * seq_dev]
    key_grad = row_dot(score_grad, query) * SCALE
    value_grad = row_dot(prob_low, grad)
    last = pl.num_programs(1) - 1

    @pl.when(pl.program_id(1) > 0)
    def _():
        total_ref[:, :HEAD_DIM] += key_grad
        total_ref[:, HEAD_DIM:] += value_grad

    @pl.when(pl.program_id(1) == 0)
    def _():
        total_ref[:, :HEAD_DIM] = key_grad
        total_ref[:, HEAD_DIM:] = value_grad

    @pl.when(pl.program_id(1) == last)
    def _():
        gkv_ref[0] = total_ref[...].astype(LOW)


def attention_call(kernel, outs, scalars, rows, keys, key_pos, seq_dev, flops):
    slots, key_count, _ = keys.shape
    heads_dev = rows[0].shape[1] // HEAD_DIM
    heads = max(1, min(heads_dev, heads_dev * 1024 // key_count))
    row_spec = pl.BlockSpec((seq_dev, heads * HEAD_DIM), lambda s, g, *_: (s, g))
    key_spec = pl.BlockSpec((1, key_count, 2 * HEAD_DIM), lambda s, g, *_: (s, 0, 0))
    pos_spec = pl.BlockSpec((1, key_count), lambda s, g, *_: (0, 0))
    shapes = {
        "row": (jax.ShapeDtypeStruct(rows[0].shape, LOW), row_spec),
        "key": (jax.ShapeDtypeStruct(keys.shape, LOW), key_spec),
    }
    return pl.pallas_call(
        partial(kernel, heads),
        grid_spec=pltpu.PrefetchScalarGridSpec(
            num_scalar_prefetch=1,
            grid=(slots, heads_dev // heads),
            in_specs=[row_spec] * len(rows) + [key_spec, pos_spec],
            out_specs=[shapes[o][1] for o in outs],
            scratch_shapes=[pltpu.VMEM(keys.shape[1:], jnp.float32) for o in outs if o == "key"],
        ),
        out_shape=[shapes[o][0] for o in outs],
        compiler_params=pltpu.CompilerParams(vmem_limit_bytes=50 * 1024 * 1024),
        cost_estimate=pl.CostEstimate(
            flops=flops * slots * heads_dev * seq_dev * key_count * HEAD_DIM * 2,
            bytes_accessed=8 * 1024 * 1024,
            transcendentals=slots * heads_dev * seq_dev * key_count,
        ),
    )(scalars, *rows, keys, key_pos)


def at(index, count):
    return pl.ds(pl.multiple_of(index * count, count), count)


def put_lines(ref, start, lines):
    first = lines.astype(LOW)
    count = lines.shape[0]
    ref[start : start + count] = first
    ref[start + count : start + 2 * count] = (lines - wide(first)).astype(LOW)


def get_lines(ref, start):
    count = (ref.shape[0] - start) // 2
    return wide(ref[start : start + count]) + wide(ref[start + count : start + 2 * count])


def first_stage(where, in_ref, grad_ref, lines_ref, send_ref, keep_ref, total_ref):
    total_ref[...] = row_dot(in_ref[...], grad_ref[...])
    count = keep_ref.shape[0]
    send_ref[:count] = total_ref[at(1 - where[0], count)].astype(LOW)
    keep_ref[...] = total_ref[at(where[0], count)]
    put_lines(send_ref, count, lines_ref[...])


def plane_stage(where, got_ref, sent_ref, keep_ref, *rest):
    *sends, mine_ref, total_ref = rest
    count, part = keep_ref.shape[0], mine_ref.shape[0]
    total_ref[...] = keep_ref[...] + wide(got_ref[:count])
    lines = get_lines(sent_ref, count) + get_lines(got_ref, count)
    mine_ref[...] = total_ref[at(where[1], part)]
    for i, send in enumerate(sends):
        send[:part] = total_ref[at(where[2 + i], part)].astype(LOW)
        put_lines(send, part, lines)


def plane_sum(x_ref, y_ref, xy_ref, sent_ref, mine_ref, send_ref):
    part = mine_ref.shape[0]
    total = mine_ref[...] + wide(x_ref[:part]) + wide(y_ref[:part]) + wide(xy_ref[:part])
    send_ref[:part] = total.astype(LOW)
    lines = get_lines(sent_ref, part) + get_lines(x_ref, part)
    put_lines(send_ref, part, lines + (get_lines(y_ref, part) + get_lines(xy_ref, part)))


def pair_sum(part, got_ref, sent_ref, send_ref):
    send_ref[:part] = (wide(sent_ref[:part]) + wide(got_ref[:part])).astype(LOW)
    put_lines(send_ref, part, get_lines(sent_ref, part) + get_lines(got_ref, part))


def last_sum(part, got_ref, sent_ref, rows_ref, lines_ref):
    rows_ref[...] = (wide(sent_ref[:part]) + wide(got_ref[:part])).astype(LOW)
    lines_ref[...] = get_lines(sent_ref, part) + get_lines(got_ref, part)


def join_stage(first, where, *refs):
    *parts, whole_ref = refs
    for i, part in enumerate(parts):
        whole_ref[at(where[first + i], part.shape[0])] = part[...].astype(whole_ref.dtype)


def small_call(kernel, outs, *args, scratch=(), where=None):
    lead = [] if where is None else [where]
    specs = [pl.BlockSpec(memory_space=pltpu.SMEM)] * len(lead)
    return pl.pallas_call(
        kernel,
        in_specs=specs + [pl.BlockSpec(memory_space=pltpu.VMEM)] * len(args),
        out_specs=[pl.BlockSpec(memory_space=pltpu.VMEM)] * len(outs),
        out_shape=[jax.ShapeDtypeStruct(*o) for o in outs],
        scratch_shapes=[pltpu.VMEM(*v) for v in scratch],
        compiler_params=pltpu.CompilerParams(vmem_limit_bytes=24 * 1024 * 1024),
        cost_estimate=pl.CostEstimate(
            flops=1024 * 1024, bytes_accessed=2 * 1024 * 1024, transcendentals=0
        ),
    )(*lead, *args)


def on_device(
    block_in,
    lengths,
    out_cot,
    ln1_gain,
    ln1_bias,
    w_q,
    b_q,
    w_kv,
    b_v,
    w_out,
    b_out,
    ln2_gain,
    ln2_bias,
    w_up,
    b_up,
    w_down,
    b_down,
):
    blk_count = lax.axis_size("blk")
    blk = lax.axis_index("blk")
    head = lax.axis_index("head")
    z_count = blk_count // 2
    z, x = blk // 2, blk % 2
    y, core = head // 2, head % 2
    slots = lax.axis_size("head")
    seq_dev = block_in.shape[1]
    width = block_in.shape[2]
    depth = w_q.shape[0]
    q_dev = w_q.shape[1]
    ff_dev = w_up.shape[1]
    unit = ff_dev // 2
    part_unit = unit // 2
    plane = [(0, 2), (1, 0), (1, 2)]
    z_groups = [[2 * i + j for i in range(z_count)] for j in range(2)]

    def gather_z(values):
        return lax.all_gather(values, "blk", axis=0, axis_index_groups=z_groups)

    def scatter_z(values):
        return lax.psum_scatter(
            values, "blk", scatter_dimension=0, axis_index_groups=z_groups
        )

    def pair_y(values):
        return jnp.stack([values, flip(values, head_bits=2)])

    def pair_core(pair):
        return jnp.concatenate([pair, flip(pair, head_bits=1)])

    def gather_head(values):
        return pair_core(pair_y(values))

    def add_core(left, right):
        rows = left[0].shape[0] // 2
        send = sum(col_dot(v[rows:], w) for v, w in zip(left, right))
        keep = sum(col_dot(v[:rows], w) for v, w in zip(left, right))
        keep = keep + wide(flip(low(send), head_bits=1))
        return keep.reshape(-1, seq_dev, width)

    def add_y(half):
        return half[0] + wide(flip(low(half[1]), head_bits=2))

    def gather_xy(values):
        return jnp.stack([values] + [flip(values, *bits) for bits in plane])

    def gather_core(mine):
        return jnp.concatenate([mine, flip(mine, head_bits=1)]).reshape(-1, width)

    def plane_xy(half):
        total = half[0]
        for i, bits in enumerate(plane):
            total = total + wide(flip(low(half[i + 1]), *bits))
        return total

    def swap_units(weights):
        own = lax.dynamic_slice_in_dim(weights, x * unit, unit, 1)
        other = lax.dynamic_slice_in_dim(weights, (1 - x) * unit, unit, 1)
        return in_order(own, flip(other, blk_bits=1), x, 0).reshape(2 * depth, unit)

    def gather_x(mine):
        return in_order(mine, flip(mine, blk_bits=1), x, 1).reshape(width, -1)

    mine = gather_z(jnp.concatenate([w_q, w_out]))
    mine_q, mine_out = mine[:, :depth], mine[:, depth:]
    full_q = gather_x(mine_q)
    def gather_units(mine):
        return [
            gather_z(mine[:, i * part_unit : (i + 1) * part_unit]).reshape(width, part_unit)
            for i in range(2)
        ]

    full_up = gather_units(swap_units(w_up))
    mine_down = swap_units(w_down)

    own_rows = wide(block_in[0])
    positions = jnp.arange(seq_dev, dtype=jnp.int32)
    own_valid = blk * seq_dev + positions < lengths[head]
    attn_in = layer_norm(own_rows, ln1_gain, ln1_bias).astype(LOW)
    value_bias = jnp.concatenate([jnp.zeros((HEAD_DIM,), jnp.float32), b_v])
    keys = (plain_dot(attn_in, w_kv) + value_bias).astype(LOW)[None]
    bit = blk_count // 2
    while bit:
        keys = jnp.stack([keys, flip(keys, blk_bits=bit)], axis=1)
        keys = keys.reshape((-1,) + keys.shape[2:])
        bit //= 2
    keys, mine_down = tie(keys, mine_down)
    full_down = gather_z(mine_down).reshape(width, unit)
    keys = gather_head(keys).reshape(slots, blk_count * seq_dev, 2 * HEAD_DIM)
    key_blocks = blk ^ jnp.arange(blk_count, dtype=jnp.int32)
    key_pos = (key_blocks[:, None] * seq_dev + positions[None, :]).reshape(1, -1)
    slot_ids = head ^ jnp.array([0, 2, 1, 3], jnp.int32)
    scalars = jnp.concatenate([(blk * seq_dev)[None], lengths[slot_ids]]).astype(jnp.int32)
    group_in = gather_head(attn_in).reshape(slots * seq_dev, width)

    own_cot = jnp.where(own_valid[:, None], out_cot[0], jnp.zeros_like(out_cot[0]))
    cot_mine = pair_y(own_cot)
    own_cot = wide(own_cot)

    column_start = head * q_dev
    query_bias = lax.dynamic_slice_in_dim(b_q, column_start, q_dev)
    queries = (plain_dot(group_in, full_q) + query_bias).astype(LOW)
    queries, mine_out, cot_mine = tie(queries, mine_out, cot_mine)
    full_out = gather_x(mine_out)
    (attn_low,) = attention_call(
        forward_kernel, ("row",), scalars, (queries,), keys, key_pos, seq_dev, 2
    )
    attn_low, full_up[0], cot_mine = tie(attn_low, full_up[0], cot_mine)
    cot_rows = gather_core(jnp.concatenate([cot_mine, flip(cot_mine, blk_bits=1)]))
    hidden_res = own_rows + add_y(add_core([attn_low], [full_out])) + b_out
    hidden_res, full_up[1], cot_rows = tie(hidden_res, full_up[1], cot_rows)
    normed_two = layer_norm(hidden_res, ln2_gain, ln2_bias).astype(LOW)
    ffn_in = gather_core(gather_xy(normed_two))
    unit_start = head * ff_dev + x * unit

    def gelu(i):
        bias = lax.dynamic_slice_in_dim(b_up, unit_start + i * part_unit, part_unit)
        value, pull = jax.vjp(
            partial(jax.nn.gelu, approximate=True), plain_dot(ffn_in, full_up[i]) + bias
        )
        return low(value), pull

    def ff_send(sums):
        parts = jnp.concatenate(sums, axis=-1).reshape(2, depth, unit)
        return take(parts, x, 0), flip(take(parts, 1 - x, 0), blk_bits=1)

    def ff_join(own, other):
        first = x == 0
        return wide(
            jnp.concatenate([jnp.where(first, own, other), jnp.where(first, other, own)], axis=-1)
        )

    def scatter_units(grads):
        return scatter_z(grads.reshape(z_count, 2 * depth, part_unit))

    activated, gelu_pulls = zip(*[gelu(i) for i in range(2)])
    activated = tie(*activated)
    grad_down = [low(row_dot(cot_rows, v)) for v in activated]

    *grad_down, full_down = tie(*grad_down, full_down)
    sums_down = [scatter_units(grad_down[0])]
    grad_act = plain_dot(cot_rows, full_down)
    grad_up_rows = [
        low(gelu_pulls[i](grad_act[:, i * part_unit : (i + 1) * part_unit])[0]) for i in range(2)
    ]
    in_half = add_core(grad_up_rows, full_up)
    in_half, activated, grad_up_rows, grad_down = tie(
        in_half, activated, grad_up_rows, grad_down[1]
    )
    sums_down.append(scatter_units(grad_down))
    ffn_in_grad = plane_xy(in_half)
    grad_up = [low(row_dot(ffn_in, v)) for v in grad_up_rows]
    ffn_in_grad, sums_down[0], grad_up, activated = tie(
        ffn_in_grad, sums_down[0], grad_up, activated
    )
    ffn_half = add_core([jnp.concatenate(activated, axis=-1)], [full_down])
    sums_up = [scatter_units(v) for v in grad_up]
    grad_up_bias = jnp.concatenate(
        [jnp.sum(v, axis=0, dtype=jnp.float32) for v in grad_up_rows]
    )

    norm_two_value, norm_two_pull = jax.vjp(layer_norm, hidden_res, ln2_gain, ln2_bias)
    res_grad, grad_ln2_gain, grad_ln2_bias = norm_two_pull(ffn_in_grad)
    res_total = own_cot + res_grad

    cot_pair, ffn_half = tie(pair_y(low(res_total)), ffn_half)
    cot_attn = pair_core(cot_pair).reshape(slots * seq_dev, width)
    attn_grad = plain_dot(cot_attn, full_out).astype(LOW)
    query_low, kv_grad = attention_call(
        backward_kernel,
        ("row", "key"),
        scalars,
        (queries, attn_grad),
        keys,
        key_pos,
        seq_dev,
        5,
    )
    kv_grad = kv_grad.reshape(slots, blk_count, seq_dev, 2 * HEAD_DIM)
    half_kv = wide(kv_grad[:2]) + wide(flip(kv_grad[2:], head_bits=1))
    half_kv, query_low, cot_late, in_late, sums_down[1] = tie(
        half_kv, query_low, cot_attn, group_in, sums_down[1]
    )
    half_in = add_core([query_low], [full_q])

    def sides(grads):
        parts = grads.reshape(z_count, 2, depth, q_dev)
        return take(parts, x, 1), low(take(parts, 1 - x, 1))

    grad_q, q_across = sides(row_dot(in_late, query_low))
    q_across = flip(q_across, blk_bits=1)
    part, half_in, grad_q, cot_late = tie(add_y(half_kv), half_in, grad_q, cot_late)
    grad_out, out_across = sides(row_dot(cot_late, attn_low))
    bit = 1
    while bit < blk_count:
        pair = part.reshape((-1, 2) + part.shape[1:])
        part = pair[:, 0] + wide(flip(low(pair[:, 1]), blk_bits=bit))
        if bit == 1:
            part, grad_out, out_across, q_across, sums_up[0] = tie(
                part, grad_out, out_across, q_across, sums_up[0]
            )
            out_across = flip(out_across, blk_bits=1)
        bit *= 2
    own_kv_grad, grad_q, sums_down = tie(low(part[0]), grad_q, sums_down)
    sum_q = wide(scatter_z(low(grad_q + wide(q_across))))
    down_own, down_other = ff_send(sums_down)
    norm_one_grad = add_y(half_in) + col_dot(own_kv_grad, w_kv)
    norm_one_value, norm_one_pull = jax.vjp(layer_norm, own_rows, ln1_gain, ln1_bias)
    input_part, grad_ln1_gain, grad_ln1_bias = norm_one_pull(norm_one_grad)
    input_grad = res_total + input_part

    grad_b_q = lax.dynamic_update_slice_in_dim(
        jnp.zeros((width,), jnp.float32),
        jnp.sum(query_low, axis=0, dtype=jnp.float32),
        column_start,
        0,
    )
    grad_b_up = lax.dynamic_update_slice_in_dim(jnp.zeros_like(b_up), grad_up_bias, unit_start, 0)
    grad_b_v = jnp.sum(own_kv_grad[:, HEAD_DIM:], axis=0, dtype=jnp.float32)
    lines = jnp.concatenate(
        [
            jnp.stack(
                [
                    grad_ln1_gain,
                    grad_ln1_bias,
                    grad_b_q,
                    jnp.sum(res_total, axis=0),
                    grad_ln2_gain,
                    grad_ln2_bias,
                    jnp.sum(own_cot, axis=0),
                    jnp.pad(grad_b_v, (0, width - HEAD_DIM)),
                ]
            ),
            grad_b_up.reshape(-1, width),
        ]
    ).reshape(-1, 2 * HEAD_DIM)
    line_count = lines.shape[0]

    columns = 2 * HEAD_DIM
    rows_half, rows_part = width // 2, width // 8
    message = (rows_part + 2 * line_count, columns)
    where = jnp.stack(
        [core, 2 * x + y, 2 * x + 1 - y, 2 * (1 - x) + y, 2 * (1 - x) + 1 - y, core, 1 - core]
    ).astype(jnp.int32)
    sent, keep = small_call(
        first_stage,
        [((rows_half + 2 * line_count, columns), LOW), ((rows_half, columns), jnp.float32)],
        attn_in,
        own_kv_grad,
        lines,
        scratch=[((width, columns), jnp.float32)],
        where=where,
    )
    *sent, keep = small_call(
        plane_stage,
        [(message, LOW)] * 3 + [((rows_part, columns), jnp.float32)],
        flip(sent, head_bits=1),
        sent,
        keep,
        scratch=[((rows_half, columns), jnp.float32)],
        where=where,
    )
    got = [flip(v, *bits) for v, bits in zip(sent, plane)]
    (sent,) = small_call(plane_sum, [(message, LOW)], *got, sent[0], keep)
    sent, ffn_half, out_across, sums_up[1], down_own = tie(
        sent, ffn_half, out_across, sums_up[1], down_own
    )
    sum_down = ff_join(down_own, down_other)
    up_own, up_other = ff_send(sums_up)
    ffn_got = [flip(low(ffn_half[i + 1]), *bits) for i, bits in enumerate(plane)]
    sum_out = wide(scatter_z(low(grad_out + wide(out_across))))
    bit = 2
    while 2 * bit < blk_count:
        (sent,) = small_call(
            partial(pair_sum, rows_part), [(message, LOW)], flip(sent, blk_bits=bit), sent
        )
        bit *= 2
    rows, lines = small_call(
        partial(last_sum, rows_part),
        [((rows_part, columns), LOW), ((line_count, columns), jnp.float32)],
        flip(sent, blk_bits=bit),
        sent,
    )
    rows, sum_q, up_other, ffn_got = tie(rows, sum_q, up_other, ffn_got)
    (rows,) = small_call(
        partial(join_stage, 1),
        [((rows_half, columns), LOW)],
        rows,
        *[flip(rows, *bits) for bits in plane],
        where=where,
    )
    rows, up_own, ffn_total = tie(rows, up_own, ffn_half[0])
    sum_up = ff_join(up_own, up_other)
    output = low(hidden_res + ffn_total + sum(wide(v) for v in ffn_got) + b_down)[None]
    (sum_kv,) = small_call(
        partial(join_stage, 5),
        [((width, columns), jnp.float32)],
        rows,
        flip(rows, head_bits=1),
        where=where,
    )
    lines = lines.reshape(-1, width)
    (
        sum_ln1_gain,
        sum_ln1_bias,
        sum_q_bias,
        sum_out_bias,
        sum_ln2_gain,
        sum_ln2_bias,
        sum_down_bias,
        sum_v_bias,
    ) = lines[:8]
    sum_v_bias = sum_v_bias[:HEAD_DIM]
    sum_up_bias = lines[8:].reshape(-1)
    return (
        output,
        input_grad[None],
        sum_ln1_gain,
        sum_ln1_bias,
        sum_q,
        sum_q_bias,
        sum_kv,
        sum_v_bias,
        sum_out,
        sum_out_bias,
        sum_ln2_gain,
        sum_ln2_bias,
        sum_up,
        sum_up_bias,
        sum_down,
        sum_down_bias,
    )


def solution(mesh):
    rows = P("head", "blk", None)
    weights = P("blk", "head")
    in_specs = (
        rows,
        P(),
        rows,
        P(),
        P(),
        weights,
        P(),
        P(),
        P(),
        weights,
        P(),
        P(),
        P(),
        weights,
        P(),
        weights,
        P(),
    )
    out_specs = (
        rows,
        rows,
        P(),
        P(),
        weights,
        P(),
        P(),
        P(),
        weights,
        P(),
        P(),
        P(),
        weights,
        P(),
        weights,
        P(),
    )
    return jax.shard_map(
        on_device, mesh=mesh, in_specs=in_specs, out_specs=out_specs, check_vma=False
    )
```

```python
from functools import partial

import jax
import jax.numpy as jnp
from jax import lax
from jax.experimental import pallas as pl
from jax.experimental.pallas import tpu as pltpu
from jax.sharding import PartitionSpec as P

HEADS = 16
HEAD_DIM = 128
EPSILON = 1e-05
SCALE = HEAD_DIM ** (-0.5)
LOW = jnp.bfloat16


def layer_norm(values, gain, bias):
    center = values - jnp.mean(values, axis=-1, keepdims=True)
    spread = jnp.mean(center * center, axis=-1, keepdims=True)
    return center * lax.rsqrt(spread + EPSILON) * gain + bias


def plain_dot(left, right):
    return jnp.dot(left, right, preferred_element_type=jnp.float32)


def row_dot(left, right):
    return lax.dot_general(
        left, right, (((0,), (0,)), ((), ())), preferred_element_type=jnp.float32
    )


def col_dot(left, right):
    return lax.dot_general(
        left, right, (((1,), (1,)), ((), ())), preferred_element_type=jnp.float32
    )


def wide(values):
    return values.astype(jnp.float32)


def low(values):
    return values.astype(LOW)


def rounded(values):
    return lax.reduce_precision(values, 8, 7)


def flip(values, blk_bits=0, head_bits=0):
    blk_count = lax.axis_size("blk")
    head_count = lax.axis_size("head")
    pairs = [
        (b * head_count + h, (b ^ blk_bits) * head_count + (h ^ head_bits))
        for b in range(blk_count)
        for h in range(head_count)
    ]
    return lax.ppermute(values, ("blk", "head"), pairs)


def in_order(own, other, index, axis):
    first = index == 0
    return jnp.stack([jnp.where(first, own, other), jnp.where(first, other, own)], axis=axis)


def tie(*values):
    return lax.optimization_barrier(values)


def take(values, index, axis):
    return lax.dynamic_index_in_dim(values, index, axis, keepdims=False)


def stacked(ref, heads):
    return jnp.concatenate(
        [ref[:, h * HEAD_DIM : (h + 1) * HEAD_DIM] for h in range(heads)], axis=0
    )


def probabilities(query, key, key_pos, start, length, seq_dev):
    raw = col_dot(query, key) * SCALE
    row = lax.broadcasted_iota(jnp.int32, (query.shape[0], 1), 0)
    row_pos = start + row % seq_dev
    limit = jnp.minimum(row_pos, length - 1)
    masked = jnp.where(key_pos <= limit, raw, -1e30)
    weights = jnp.exp(masked - jnp.max(masked, axis=-1, keepdims=True))
    return weights * (1.0 / jnp.sum(weights, axis=-1, keepdims=True))


def forward_kernel(heads, scalars, q_ref, kv_ref, pos_ref, o_ref):
    seq_dev = q_ref.shape[0]
    key = kv_ref[0, :, :HEAD_DIM]
    value = kv_ref[0, :, HEAD_DIM:]
    prob = probabilities(
        stacked(q_ref, heads),
        key,
        pos_ref[...],
        scalars[0],
        scalars[1 + pl.program_id(0)],
        seq_dev,
    )
    out = plain_dot(prob.astype(LOW), value).astype(LOW)
    for h in range(heads):
        o_ref[:, h * HEAD_DIM : (h + 1) * HEAD_DIM] = out[h * seq_dev : (h + 1) * seq_dev]


def backward_kernel(heads, scalars, q_ref, go_ref, kv_ref, pos_ref, gq_ref, gkv_ref, total_ref):
    seq_dev = q_ref.shape[0]
    key = kv_ref[0, :, :HEAD_DIM]
    value = kv_ref[0, :, HEAD_DIM:]
    query = stacked(q_ref, heads)
    grad = stacked(go_ref, heads)
    prob = probabilities(
        query,
        key,
        pos_ref[...],
        scalars[0],
        scalars[1 + pl.program_id(0)],
        seq_dev,
    )
    prob_low = prob.astype(LOW)
    prob_grad = col_dot(grad, value)
    delta = jnp.sum(wide(prob_low) * prob_grad, axis=-1, keepdims=True)
    score_grad = (prob * (prob_grad - delta)).astype(LOW)
    out = (plain_dot(score_grad, key) * SCALE).astype(LOW)
    for h in range(heads):
        gq_ref[:, h * HEAD_DIM : (h + 1) * HEAD_DIM] = out[h * seq_dev : (h + 1) * seq_dev]
    key_grad = row_dot(score_grad, query) * SCALE
    value_grad = row_dot(prob_low, grad)
    last = pl.num_programs(1) - 1

    @pl.when(pl.program_id(1) > 0)
    def _():
        total_ref[:, :HEAD_DIM] += key_grad
        total_ref[:, HEAD_DIM:] += value_grad

    @pl.when(pl.program_id(1) == 0)
    def _():
        total_ref[:, :HEAD_DIM] = key_grad
        total_ref[:, HEAD_DIM:] = value_grad

    @pl.when(pl.program_id(1) == last)
    def _():
        gkv_ref[0] = total_ref[...].astype(LOW)


def attention_call(kernel, outs, scalars, rows, keys, key_pos, seq_dev, flops):
    slots, key_count, _ = keys.shape
    heads_dev = rows[0].shape[1] // HEAD_DIM
    heads = max(1, min(heads_dev, heads_dev * 1024 // key_count))
    row_spec = pl.BlockSpec((seq_dev, heads * HEAD_DIM), lambda s, g, *_: (s, g))
    key_spec = pl.BlockSpec((1, key_count, 2 * HEAD_DIM), lambda s, g, *_: (s, 0, 0))
    pos_spec = pl.BlockSpec((1, key_count), lambda s, g, *_: (0, 0))
    shapes = {
        "row": (jax.ShapeDtypeStruct(rows[0].shape, LOW), row_spec),
        "key": (jax.ShapeDtypeStruct(keys.shape, LOW), key_spec),
    }
    return pl.pallas_call(
        partial(kernel, heads),
        grid_spec=pltpu.PrefetchScalarGridSpec(
            num_scalar_prefetch=1,
            grid=(slots, heads_dev // heads),
            in_specs=[row_spec] * len(rows) + [key_spec, pos_spec],
            out_specs=[shapes[o][1] for o in outs],
            scratch_shapes=[pltpu.VMEM(keys.shape[1:], jnp.float32) for o in outs if o == "key"],
        ),
        out_shape=[shapes[o][0] for o in outs],
        compiler_params=pltpu.CompilerParams(vmem_limit_bytes=50 * 1024 * 1024),
        cost_estimate=pl.CostEstimate(
            flops=flops * slots * heads_dev * seq_dev * key_count * HEAD_DIM * 2,
            bytes_accessed=8 * 1024 * 1024,
            transcendentals=slots * heads_dev * seq_dev * key_count,
        ),
    )(scalars, *rows, keys, key_pos)


def at(index, count):
    return pl.ds(pl.multiple_of(index * count, count), count)


def put_lines(ref, start, lines):
    first = lines.astype(LOW)
    count = lines.shape[0]
    ref[start : start + count] = first
    ref[start + count : start + 2 * count] = (lines - wide(first)).astype(LOW)


def get_lines(ref, start):
    count = (ref.shape[0] - start) // 2
    return wide(ref[start : start + count]) + wide(ref[start + count : start + 2 * count])


def first_stage(where, in_ref, grad_ref, lines_ref, send_ref, keep_ref, total_ref):
    total_ref[...] = row_dot(in_ref[...], grad_ref[...])
    count = keep_ref.shape[0]
    send_ref[:count] = total_ref[at(1 - where[0], count)].astype(LOW)
    keep_ref[...] = total_ref[at(where[0], count)]
    put_lines(send_ref, count, lines_ref[...])


def plane_stage(where, got_ref, sent_ref, keep_ref, *rest):
    *sends, mine_ref, total_ref = rest
    count, part = keep_ref.shape[0], mine_ref.shape[0]
    total_ref[...] = keep_ref[...] + wide(got_ref[:count])
    lines = get_lines(sent_ref, count) + get_lines(got_ref, count)
    mine_ref[...] = total_ref[at(where[1], part)]
    for i, send in enumerate(sends):
        send[:part] = total_ref[at(where[2 + i], part)].astype(LOW)
        put_lines(send, part, lines)


def plane_sum(x_ref, y_ref, xy_ref, sent_ref, mine_ref, send_ref):
    part = mine_ref.shape[0]
    total = mine_ref[...] + wide(x_ref[:part]) + wide(y_ref[:part]) + wide(xy_ref[:part])
    send_ref[:part] = total.astype(LOW)
    lines = get_lines(sent_ref, part) + get_lines(x_ref, part)
    put_lines(send_ref, part, lines + (get_lines(y_ref, part) + get_lines(xy_ref, part)))


def pair_sum(part, got_ref, sent_ref, send_ref):
    send_ref[:part] = (wide(sent_ref[:part]) + wide(got_ref[:part])).astype(LOW)
    put_lines(send_ref, part, get_lines(sent_ref, part) + get_lines(got_ref, part))


def last_sum(part, got_ref, sent_ref, rows_ref, lines_ref):
    rows_ref[...] = (wide(sent_ref[:part]) + wide(got_ref[:part])).astype(LOW)
    lines_ref[...] = get_lines(sent_ref, part) + get_lines(got_ref, part)


def join_stage(first, where, *refs):
    *parts, whole_ref = refs
    for i, part in enumerate(parts):
        whole_ref[at(where[first + i], part.shape[0])] = part[...].astype(whole_ref.dtype)


def small_call(kernel, outs, *args, scratch=(), where=None):
    lead = [] if where is None else [where]
    specs = [pl.BlockSpec(memory_space=pltpu.SMEM)] * len(lead)
    return pl.pallas_call(
        kernel,
        in_specs=specs + [pl.BlockSpec(memory_space=pltpu.VMEM)] * len(args),
        out_specs=[pl.BlockSpec(memory_space=pltpu.VMEM)] * len(outs),
        out_shape=[jax.ShapeDtypeStruct(*o) for o in outs],
        scratch_shapes=[pltpu.VMEM(*v) for v in scratch],
        compiler_params=pltpu.CompilerParams(vmem_limit_bytes=24 * 1024 * 1024),
        cost_estimate=pl.CostEstimate(
            flops=1024 * 1024, bytes_accessed=2 * 1024 * 1024, transcendentals=0
        ),
    )(*lead, *args)


def on_device(
    block_in,
    lengths,
    out_cot,
    ln1_gain,
    ln1_bias,
    w_q,
    b_q,
    w_kv,
    b_v,
    w_out,
    b_out,
    ln2_gain,
    ln2_bias,
    w_up,
    b_up,
    w_down,
    b_down,
):
    blk_count = lax.axis_size("blk")
    blk = lax.axis_index("blk")
    head = lax.axis_index("head")
    z_count = blk_count // 2
    z, x = blk // 2, blk % 2
    y, core = head // 2, head % 2
    slots = lax.axis_size("head")
    seq_dev = block_in.shape[1]
    width = block_in.shape[2]
    depth = w_q.shape[0]
    q_dev = w_q.shape[1]
    ff_dev = w_up.shape[1]
    unit = ff_dev // 2
    part_unit = unit // 2
    plane = [(0, 2), (1, 0), (1, 2)]
    z_groups = [[2 * i + j for i in range(z_count)] for j in range(2)]

    def gather_z(values):
        return lax.all_gather(values, "blk", axis=0, axis_index_groups=z_groups)

    def scatter_z(values):
        return lax.psum_scatter(
            values, "blk", scatter_dimension=0, axis_index_groups=z_groups
        )

    def pair_y(values):
        return jnp.stack([values, flip(values, head_bits=2)])

    def pair_core(pair):
        return jnp.concatenate([pair, flip(pair, head_bits=1)])

    def gather_head(values):
        return pair_core(pair_y(values))

    def add_core(left, right):
        rows = left[0].shape[0] // 2
        send = sum(col_dot(v[rows:], w) for v, w in zip(left, right))
        keep = sum(col_dot(v[:rows], w) for v, w in zip(left, right))
        keep = keep + wide(flip(low(send), head_bits=1))
        return keep.reshape(-1, seq_dev, width)

    def add_y(half):
        return half[0] + wide(flip(low(half[1]), head_bits=2))

    def gather_xy(values):
        return jnp.stack([values] + [flip(values, *bits) for bits in plane])

    def gather_core(mine):
        return jnp.concatenate([mine, flip(mine, head_bits=1)]).reshape(-1, width)

    def plane_xy(half):
        total = half[0]
        for i, bits in enumerate(plane):
            total = total + wide(flip(low(half[i + 1]), *bits))
        return total

    def swap_units(weights):
        own = lax.dynamic_slice_in_dim(weights, x * unit, unit, 1)
        other = lax.dynamic_slice_in_dim(weights, (1 - x) * unit, unit, 1)
        return in_order(own, flip(other, blk_bits=1), x, 0).reshape(2 * depth, unit)

    def gather_x(mine):
        return in_order(mine, flip(mine, blk_bits=1), x, 1).reshape(width, -1)

    mine = gather_z(jnp.concatenate([w_q, w_out]))
    mine_q, mine_out = mine[:, :depth], mine[:, depth:]
    full_q = gather_x(mine_q)
    def gather_units(mine):
        return [
            gather_z(mine[:, i * part_unit : (i + 1) * part_unit]).reshape(width, part_unit)
            for i in range(2)
        ]

    full_up = gather_units(swap_units(w_up))
    mine_down = swap_units(w_down)

    own_rows = wide(block_in[0])
    positions = jnp.arange(seq_dev, dtype=jnp.int32)
    own_valid = blk * seq_dev + positions < lengths[head]
    attn_in = layer_norm(own_rows, ln1_gain, ln1_bias).astype(LOW)
    value_bias = jnp.concatenate([jnp.zeros((HEAD_DIM,), jnp.float32), b_v])
    keys = (plain_dot(attn_in, w_kv) + value_bias).astype(LOW)[None]
    bit = blk_count // 2
    while bit:
        keys = jnp.stack([keys, flip(keys, blk_bits=bit)], axis=1)
        keys = keys.reshape((-1,) + keys.shape[2:])
        bit //= 2
    keys, mine_down = tie(keys, mine_down)
    full_down = gather_z(mine_down).reshape(width, unit)
    keys = gather_head(keys).reshape(slots, blk_count * seq_dev, 2 * HEAD_DIM)
    key_blocks = blk ^ jnp.arange(blk_count, dtype=jnp.int32)
    key_pos = (key_blocks[:, None] * seq_dev + positions[None, :]).reshape(1, -1)
    slot_ids = head ^ jnp.array([0, 2, 1, 3], jnp.int32)
    scalars = jnp.concatenate([(blk * seq_dev)[None], lengths[slot_ids]]).astype(jnp.int32)
    group_in = gather_head(attn_in).reshape(slots * seq_dev, width)

    own_cot = jnp.where(own_valid[:, None], out_cot[0], jnp.zeros_like(out_cot[0]))
    cot_mine = pair_y(own_cot)
    own_cot = wide(own_cot)

    column_start = head * q_dev
    query_bias = lax.dynamic_slice_in_dim(b_q, column_start, q_dev)
    queries = (plain_dot(group_in, full_q) + query_bias).astype(LOW)
    queries, mine_out, cot_mine = tie(queries, mine_out, cot_mine)
    full_out = gather_x(mine_out)
    (attn_low,) = attention_call(
        forward_kernel, ("row",), scalars, (queries,), keys, key_pos, seq_dev, 2
    )
    attn_low, full_up[0], cot_mine = tie(attn_low, full_up[0], cot_mine)
    cot_rows = gather_core(jnp.concatenate([cot_mine, flip(cot_mine, blk_bits=1)]))
    hidden_res = own_rows + add_y(add_core([attn_low], [full_out])) + b_out
    hidden_res, full_up[1], cot_rows = tie(hidden_res, full_up[1], cot_rows)
    normed_two = layer_norm(hidden_res, ln2_gain, ln2_bias).astype(LOW)
    ffn_in = gather_core(gather_xy(normed_two))
    unit_start = head * ff_dev + x * unit

    def gelu(i):
        bias = lax.dynamic_slice_in_dim(b_up, unit_start + i * part_unit, part_unit)
        value, pull = jax.vjp(
            partial(jax.nn.gelu, approximate=True), plain_dot(ffn_in, full_up[i]) + bias
        )
        return low(value), pull

    def ff_send(sums):
        parts = jnp.concatenate(sums, axis=-1).reshape(2, depth, unit)
        return take(parts, x, 0), flip(take(parts, 1 - x, 0), blk_bits=1)

    def ff_join(own, other):
        first = x == 0
        return wide(
            jnp.concatenate([jnp.where(first, own, other), jnp.where(first, other, own)], axis=-1)
        )

    def scatter_units(grads):
        return scatter_z(grads.reshape(z_count, 2 * depth, part_unit))

    activated, gelu_pulls = zip(*[gelu(i) for i in range(2)])
    activated = tie(*activated)
    grad_down = [low(row_dot(cot_rows, v)) for v in activated]

    *grad_down, full_down = tie(*grad_down, full_down)
    sums_down = [scatter_units(grad_down[0])]
    grad_act = plain_dot(cot_rows, full_down)
    grad_up_rows = [
        low(gelu_pulls[i](grad_act[:, i * part_unit : (i + 1) * part_unit])[0]) for i in range(2)
    ]
    in_half = add_core(grad_up_rows, full_up)
    in_half, activated, grad_up_rows, grad_down = tie(
        in_half, activated, grad_up_rows, grad_down[1]
    )
    sums_down.append(scatter_units(grad_down))
    ffn_in_grad = plane_xy(in_half)
    grad_up = [low(row_dot(ffn_in, v)) for v in grad_up_rows]
    ffn_in_grad, sums_down[0], grad_up, activated = tie(
        ffn_in_grad, sums_down[0], grad_up, activated
    )
    ffn_half = add_core([jnp.concatenate(activated, axis=-1)], [full_down])
    sums_up = [scatter_units(v) for v in grad_up]
    grad_up_bias = jnp.concatenate(
        [jnp.sum(v, axis=0, dtype=jnp.float32) for v in grad_up_rows]
    )

    norm_two_value, norm_two_pull = jax.vjp(layer_norm, hidden_res, ln2_gain, ln2_bias)
    res_grad, grad_ln2_gain, grad_ln2_bias = norm_two_pull(ffn_in_grad)
    res_total = own_cot + res_grad

    cot_pair, ffn_half = tie(pair_y(low(res_total)), ffn_half)
    cot_attn = pair_core(cot_pair).reshape(slots * seq_dev, width)
    attn_grad = plain_dot(cot_attn, full_out).astype(LOW)
    query_low, kv_grad = attention_call(
        backward_kernel,
        ("row", "key"),
        scalars,
        (queries, attn_grad),
        keys,
        key_pos,
        seq_dev,
        5,
    )
    kv_grad = kv_grad.reshape(slots, blk_count, seq_dev, 2 * HEAD_DIM)
    half_kv = wide(kv_grad[:2]) + wide(flip(kv_grad[2:], head_bits=1))
    half_kv, query_low, cot_late, in_late, sums_down[1] = tie(
        half_kv, query_low, cot_attn, group_in, sums_down[1]
    )
    half_in = add_core([query_low], [full_q])

    def sides(grads):
        parts = grads.reshape(z_count, 2, depth, q_dev)
        return take(parts, x, 1), low(take(parts, 1 - x, 1))

    grad_q, q_across = sides(row_dot(in_late, query_low))
    q_across = flip(q_across, blk_bits=1)
    part, half_in, grad_q, cot_late = tie(add_y(half_kv), half_in, grad_q, cot_late)
    grad_out, out_across = sides(row_dot(cot_late, attn_low))
    bit = 1
    while bit < blk_count:
        pair = part.reshape((-1, 2) + part.shape[1:])
        part = pair[:, 0] + wide(flip(low(pair[:, 1]), blk_bits=bit))
        if bit == 1:
            part, grad_out, out_across, q_across, sums_up[0] = tie(
                part, grad_out, out_across, q_across, sums_up[0]
            )
            out_across = flip(out_across, blk_bits=1)
        bit *= 2
    query_sum = jnp.sum(query_low, axis=0, dtype=jnp.float32)
    own_kv_grad, grad_q, sums_down, query_sum = tie(
        low(part[0]), grad_q, sums_down, query_sum
    )
    sum_q = wide(scatter_z(low(grad_q + wide(q_across))))
    down_own, down_other = ff_send(sums_down)
    norm_one_grad = add_y(half_in) + col_dot(own_kv_grad, w_kv)
    norm_one_value, norm_one_pull = jax.vjp(layer_norm, own_rows, ln1_gain, ln1_bias)
    input_part, grad_ln1_gain, grad_ln1_bias = norm_one_pull(norm_one_grad)
    input_grad = res_total + input_part

    grad_b_q = lax.dynamic_update_slice_in_dim(
        jnp.zeros((width,), jnp.float32),
        query_sum,
        column_start,
        0,
    )
    grad_b_up = lax.dynamic_update_slice_in_dim(jnp.zeros_like(b_up), grad_up_bias, unit_start, 0)
    grad_b_v = jnp.sum(own_kv_grad[:, HEAD_DIM:], axis=0, dtype=jnp.float32)
    lines = jnp.concatenate(
        [
            jnp.stack(
                [
                    grad_ln1_gain,
                    grad_ln1_bias,
                    grad_b_q,
                    jnp.sum(res_total, axis=0),
                    grad_ln2_gain,
                    grad_ln2_bias,
                    jnp.sum(own_cot, axis=0),
                    jnp.pad(grad_b_v, (0, width - HEAD_DIM)),
                ]
            ),
            grad_b_up.reshape(-1, width),
        ]
    ).reshape(-1, 2 * HEAD_DIM)
    line_count = lines.shape[0]

    columns = 2 * HEAD_DIM
    rows_half, rows_part = width // 2, width // 8
    message = (rows_part + 2 * line_count, columns)
    where = jnp.stack(
        [core, 2 * x + y, 2 * x + 1 - y, 2 * (1 - x) + y, 2 * (1 - x) + 1 - y, core, 1 - core]
    ).astype(jnp.int32)
    sent, keep = small_call(
        first_stage,
        [((rows_half + 2 * line_count, columns), LOW), ((rows_half, columns), jnp.float32)],
        attn_in,
        own_kv_grad,
        lines,
        scratch=[((width, columns), jnp.float32)],
        where=where,
    )
    *sent, keep = small_call(
        plane_stage,
        [(message, LOW)] * 3 + [((rows_part, columns), jnp.float32)],
        flip(sent, head_bits=1),
        sent,
        keep,
        scratch=[((rows_half, columns), jnp.float32)],
        where=where,
    )
    got = [flip(v, *bits) for v, bits in zip(sent, plane)]
    (sent,) = small_call(plane_sum, [(message, LOW)], *got, sent[0], keep)
    sent, ffn_half, out_across, sums_up[1], down_own = tie(
        sent, ffn_half, out_across, sums_up[1], down_own
    )
    sum_down = ff_join(down_own, down_other)
    up_own, up_other = ff_send(sums_up)
    ffn_got = [flip(low(ffn_half[i + 1]), *bits) for i, bits in enumerate(plane)]
    sum_out = wide(scatter_z(low(grad_out + wide(out_across))))
    bit = 2
    while 2 * bit < blk_count:
        (sent,) = small_call(
            partial(pair_sum, rows_part), [(message, LOW)], flip(sent, blk_bits=bit), sent
        )
        bit *= 2
    rows, lines = small_call(
        partial(last_sum, rows_part),
        [((rows_part, columns), LOW), ((line_count, columns), jnp.float32)],
        flip(sent, blk_bits=bit),
        sent,
    )
    rows, sum_q, up_other, ffn_got = tie(rows, sum_q, up_other, ffn_got)
    (rows,) = small_call(
        partial(join_stage, 1),
        [((rows_half, columns), LOW)],
        rows,
        *[flip(rows, *bits) for bits in plane],
        where=where,
    )
    rows, up_own, ffn_total = tie(rows, up_own, ffn_half[0])
    sum_up = ff_join(up_own, up_other)
    output = low(hidden_res + ffn_total + sum(wide(v) for v in ffn_got) + b_down)[None]
    (sum_kv,) = small_call(
        partial(join_stage, 5),
        [((width, columns), jnp.float32)],
        rows,
        flip(rows, head_bits=1),
        where=where,
    )
    lines = lines.reshape(-1, width)
    (
        sum_ln1_gain,
        sum_ln1_bias,
        sum_q_bias,
        sum_out_bias,
        sum_ln2_gain,
        sum_ln2_bias,
        sum_down_bias,
        sum_v_bias,
    ) = lines[:8]
    sum_v_bias = sum_v_bias[:HEAD_DIM]
    sum_up_bias = lines[8:].reshape(-1)
    return (
        output,
        input_grad[None],
        sum_ln1_gain,
        sum_ln1_bias,
        sum_q,
        sum_q_bias,
        sum_kv,
        sum_v_bias,
        sum_out,
        sum_out_bias,
        sum_ln2_gain,
        sum_ln2_bias,
        sum_up,
        sum_up_bias,
        sum_down,
        sum_down_bias,
    )


def solution(mesh):
    rows = P("head", "blk", None)
    weights = P("blk", "head")
    in_specs = (
        rows,
        P(),
        rows,
        P(),
        P(),
        weights,
        P(),
        P(),
        P(),
        weights,
        P(),
        P(),
        P(),
        weights,
        P(),
        weights,
        P(),
    )
    out_specs = (
        rows,
        rows,
        P(),
        P(),
        weights,
        P(),
        P(),
        P(),
        weights,
        P(),
        P(),
        P(),
        weights,
        P(),
        weights,
        P(),
    )
    return jax.shard_map(
        on_device, mesh=mesh, in_specs=in_specs, out_specs=out_specs, check_vma=False
    )
```
